32 devices in a mesh: lat: 4 (over y, x), lon: 8 (over z, core).
Axes of the slice: x: 2, y: 2, z: 4, core: 2. Of those that a mesh axis runs over, the one named last changes fastest.
Arguments:
- q_state: bfloat16 [128, 256, 1024], P(('lat', 'lon')), may hold values from -5 to 5
- scales: float32 [128, 256], P(('lat', 'lon')), may hold values from 0.1 to 2
- land_mask: int32 [256, 1024], P('lat', 'lon'), may hold values 0 or 1
- stem_weight: bfloat16 [128, 192], replicated, may hold values from -0.5 to 0.5
- stem_bias: float32 [192], replicated, may hold values from -3 to 3
- dw_weight: float32 [2, 192, 7, 7], replicated, may hold values from -0.875 to 0.875
- dw_bias: float32 [2, 192], replicated, may hold values from -3 to 3
- ln_gain: float32 [2, 192], replicated, may hold values from 0.5 to 2
- ln_bias: float32 [2, 192], replicated, may hold values from -3 to 3
- w_in: bfloat16 [2, 192, 768], replicated, may hold values from -0.4375 to 0.4375
- b_in: float32 [2, 768], replicated, may hold values from -3 to 3
- w_out: bfloat16 [2, 768, 192], replicated, may hold values from -0.21875 to 0.21875
- b_out: float32 [2, 192], replicated, may hold values from -3 to 3
- layer_scale: float32 [2, 192], replicated, may hold values from 0.3 to 1
- head_weight: bfloat16 [192, 128], replicated, may hold values from -0.4375 to 0.4375
Outputs:
- tendency: float32 [128, 256, 1024], P(None, 'lat', 'lon')
The draws below stay inside these ranges and needn't reach their ends.
Inputs may be any that keep to these rules, and one draw needn't show every extreme that they name: `land_mask`: 1 marks an ocean point, 0 a land point.
All inputs are finite; a program needn't handle non-finite values. No bound on the sum of `land_mask` on one device may be relied on, other than what follows from the above.
Results may differ from the reference program's by a relative error of at most 0.0057.
Values may be sent and summed in bfloat16 or wider, within the bound.
No kernel may reach another device: no remote copies, remote signals or barrier semaphores. Data moves between devices by JAX's collectives and lax.ppermute only.
A program may use at most 192 MiB of HBM per device.

```python
import math
import jax
import jax.numpy as jnp
from jax import lax

D = 192
HID = 768
BLOCKS = 2
LAT_DEV = 64
C_IN = 128
NLAT = 256
NLON = 1024


def with_ends(drawn, own_key, least, largest):
    index_at = [jax.random.randint(jax.random.fold_in(own_key, axis), (), 0, length) for axis, length in enumerate(drawn.shape)]
    widest = drawn.shape.index(max(drawn.shape))
    next_to = index_at[:widest] + [(index_at[widest] + 1) % drawn.shape[widest]] + index_at[widest + 1:]
    return drawn.at[tuple(index_at)].set(least).at[tuple(next_to)].set(largest)


def block_scale(rng, extent, cuts, least, top_value):
    factor_of, own = 1.0, jax.random.fold_in(rng, 6)
    for axis_at, blocks in cuts:
        steps = jnp.exp(jax.random.uniform(jax.random.fold_in(own, axis_at), (blocks,), jnp.float32, least / len(cuts), top_value / len(cuts)))
        factor_of = factor_of * jnp.repeat(steps, extent[axis_at] // blocks).reshape([-1 if axis == axis_at else 1 for axis in range(len(extent))])
    return factor_of


def centred(own_key, shape, width, reach, split=(), kind=jnp.bfloat16):
    result = jax.random.normal(own_key, shape, jnp.float32) * width
    if len(split) > 0:
        result = block_scale(own_key, shape, split, -0.22, 0.18) * result
    return jnp.clip(result, min=-reach, max=reach).astype(kind)


def setup_inputs(seed: int = 0) -> dict:
    splits = jax.random.split(jax.random.key(seed), 16)
    return {
        "q_state": centred(splits[0], (C_IN, NLAT, NLON), 1.0, 5.0, ((0, 32),)),
        "scales": jnp.clip(jnp.exp(math.log(2.0) - 2.9957323 * jax.random.uniform(splits[1], (C_IN, NLAT), jnp.float32) ** block_scale(splits[1], (C_IN, NLAT), ((0, 32),), -0.2, 0.2)), 0.1, 2.0),
        "land_mask": with_ends((jax.random.randint(splits[2], (NLAT, NLON), 0, 4) < 3).astype(jnp.int32), jax.random.fold_in(splits[2], 1), 0, 1),
        "stem_weight": centred(splits[3], (C_IN, D), C_IN ** -0.5, 0.5),
        "stem_bias": centred(splits[4], (D,), 0.5, 3.0, (), jnp.float32),
        "dw_weight": centred(splits[5], (BLOCKS, D, 7, 7), 49 ** -0.5, 0.875, (), jnp.float32),
        "dw_bias": centred(splits[6], (BLOCKS, D), 0.5, 3.0, (), jnp.float32),
        "ln_gain": jnp.clip(jnp.exp(jax.random.uniform(splits[7], (BLOCKS, D), jnp.float32, math.log(0.5), math.log(2.0))), 0.5, 2.0),
        "ln_bias": centred(splits[8], (BLOCKS, D), 0.5, 3.0, (), jnp.float32),
        "w_in": centred(splits[9], (BLOCKS, D, HID), D ** -0.5, 0.4375),
        "b_in": centred(splits[10], (BLOCKS, HID), 0.5, 3.0, (), jnp.float32),
        "w_out": centred(splits[11], (BLOCKS, HID, D), HID ** -0.5, 0.21875),
        "b_out": centred(splits[12], (BLOCKS, D), 0.5, 3.0, (), jnp.float32),
        "layer_scale": jnp.clip(jnp.exp(jax.random.uniform(splits[13], (BLOCKS, D), jnp.float32, math.log(0.3), math.log(1.0))), 0.3, 1.0),
        "head_weight": centred(splits[14], (D, C_IN), D ** -0.5, 0.4375),
    }


ln_eps = 1e-06

def depthwise(padded, kernel, shift_bias, row_count, col_count):
    summed = jnp.zeros((padded.shape[0], row_count, col_count), jnp.float32) + shift_bias[:, None, None]
    for i in range(7):
        for j in range(7):
            summed = summed + padded[:, i:i + row_count, j:j + col_count].astype(jnp.float32) * kernel[:, i, j][:, None, None]
    return summed

def mix_cells(convolved, residual_in, ocean, gain_one, lnbias_one, expand, expand_bias, contract, contract_bias, branch_scale):
    average = lax.optimization_barrier(jnp.mean(convolved, axis=0, keepdims=True))
    centered = convolved - average
    variance = lax.optimization_barrier(jnp.mean(centered * centered, axis=0, keepdims=True))
    normed = (centered * lax.rsqrt(variance + ln_eps) * gain_one[:, None] + lnbias_one[:, None]).astype(jnp.bfloat16)
    hidden = jax.nn.gelu(jnp.dot(expand.T, normed, preferred_element_type=jnp.float32) + expand_bias[:, None], approximate=False).astype(jnp.bfloat16)
    projected = jnp.dot(contract.T, hidden, preferred_element_type=jnp.float32) + contract_bias[:, None]
    updated = (residual_in.astype(jnp.float32) + branch_scale[:, None] * projected) * ocean[None, :]
    return updated.astype(jnp.bfloat16)

def pad_grid(field, margin):
    padded = jnp.pad(field, ((0, 0), (margin, margin), (0, 0)))
    return jnp.concatenate([padded[:, :, -margin:], padded, padded[:, :, :margin]], axis=2)

def reference(q_state, scales, land_mask, stem_weight, stem_bias, dw_weight, dw_bias, ln_gain, ln_bias, w_in, b_in, w_out, b_out, layer_scale, head_weight):
    state = (q_state.astype(jnp.float32) * scales[:, :, None]).astype(jnp.bfloat16)
    channels_in = state.shape[0]
    ocean = land_mask.astype(jnp.float32)
    stem_out = jnp.dot(stem_weight.T, state.reshape(channels_in, -1), preferred_element_type=jnp.float32) + stem_bias[:, None]
    features = (stem_out.reshape(-1, NLAT, NLON) * ocean[None]).astype(jnp.bfloat16)
    groups = NLAT // LAT_DEV
    for layer_index in range(BLOCKS):
        convolved = depthwise(pad_grid(features, 3), dw_weight[layer_index], dw_bias[layer_index], NLAT, NLON)
        current = features

        def band(group_index, convolved=convolved, current=current, layer_index=layer_index):
            offset = (group_index * LAT_DEV).astype(jnp.int32)
            conv_band = lax.dynamic_slice_in_dim(convolved, offset, LAT_DEV, 1).reshape(D, -1)
            feat_band = lax.dynamic_slice_in_dim(current, offset, LAT_DEV, 1).reshape(D, -1)
            ocean_band = lax.dynamic_slice_in_dim(ocean, offset, LAT_DEV, 0).reshape(-1)
            mixed = mix_cells(conv_band, feat_band, ocean_band, ln_gain[layer_index], ln_bias[layer_index], w_in[layer_index], b_in[layer_index], w_out[layer_index], b_out[layer_index], layer_scale[layer_index])
            return mixed.reshape(D, LAT_DEV, NLON)
        bands = lax.map(band, jnp.arange(groups, dtype=jnp.int32))
        features = jnp.transpose(bands, (1, 0, 2, 3)).reshape(D, NLAT, NLON)
    tendency = jnp.dot(head_weight.T, features.reshape(D, -1), preferred_element_type=jnp.float32)
    return tendency.reshape(-1, NLAT, NLON)
```

```python
import functools

import jax
import jax.numpy as jnp
from jax import lax
from jax.experimental import pallas as pl
from jax.experimental.pallas import tpu as pltpu
from jax.sharding import PartitionSpec as P

ln_eps = 1e-06
f32 = jnp.float32
bf16 = jnp.bfloat16
lanes = 128
vmem_bytes = 56 * 2**20

edge_order = [*range(0, 16), *range(48, 64), *range(16, 20), *range(44, 48)]
mid_order = [*range(24, 40), *range(40, 44), *range(20, 24)]


def params_for(flops=0, bytes_accessed=0):
    return dict(
        compiler_params=pltpu.CompilerParams(vmem_limit_bytes=vmem_bytes),
        cost_estimate=pl.CostEstimate(
            flops=int(flops), bytes_accessed=int(bytes_accessed), transcendentals=0
        ),
    )


def lane_index(shape):
    return lax.broadcasted_iota(jnp.int32, shape, len(shape) - 1)


def prep_body(q_ref, s_ref, edge_ref, mid_ref):
    channels, tiles = q_ref.shape[0], q_ref.shape[2] // lanes
    low = lax.broadcasted_iota(jnp.int32, (8, lanes), 0) < 4
    for c in range(channels):
        scale = s_ref[c]
        for b in range(tiles):
            x = q_ref[c, :, b * lanes : (b + 1) * lanes].astype(f32) * scale
            edge_ref[0, b, c, 0:16] = x[0:16].astype(bf16)
            edge_ref[0, b, c, 16:32] = x[48:64].astype(bf16)
            edge_ref[0, b, c, 32:40] = jnp.where(low, x[16:24], x[40:48]).astype(bf16)
            mid_ref[0, b, c, 0:16] = x[24:40].astype(bf16)
            mid_ref[0, b, c, 16:24] = jnp.where(low, x[40:48], x[16:24]).astype(bf16)


def prep(q_state, scales, n_lat, n_lon, rows):
    channels, n_rows, n_cols = q_state.shape
    wide = jnp.broadcast_to(scales[:, :, None], (channels, n_rows, lanes))
    sizes = (len(edge_order), len(mid_order))
    outs = pl.pallas_call(
        prep_body,
        grid=(n_lat,),
        in_specs=[
            pl.BlockSpec((channels, rows, n_cols), lambda a: (0, a, 0)),
            pl.BlockSpec((channels, rows, lanes), lambda a: (0, a, 0)),
        ],
        out_specs=[
            pl.BlockSpec((1, n_lon, channels, n, lanes), lambda a: (a, 0, 0, 0, 0)) for n in sizes
        ],
        out_shape=[
            jax.ShapeDtypeStruct((n_lat, n_lon, channels, n, lanes), bf16) for n in sizes
        ],
        name="dequantize",
        **params_for(0, 2 * q_state.size * 2),
    )(q_state, wide)
    return [o.reshape(n_lat * n_lon, channels, n, lanes) for o, n in zip(outs, sizes)]


def pack_edges(packed, row_value, slot):
    turned = row_value if slot == 0 else pltpu.roll(row_value, 8 * slot, 1)
    if packed is None:
        return turned
    here = ((lane_index(row_value.shape) + 4) >> 3) & 15
    return jnp.where(here == slot, turned, packed)


def stem_body(order, x_ref, w_ref, b_ref, mask_ref, f_ref, e_ref):
    count = len(order)
    bias = b_ref[...]
    done = 0
    while done < count:
        size = min(16, count - done)
        x = x_ref[:, done : done + size, :]
        if size == 16:
            x = jnp.swapaxes(x, 0, 1)
        else:
            x = jnp.swapaxes(x.astype(f32), 0, 1).astype(bf16)
        packed = None
        for half in range(0, size, 8):
            joined = jnp.concatenate([x[half + i] for i in range(8)], axis=1)
            y = jnp.dot(w_ref[...], joined, preferred_element_type=f32)
            for i in range(8):
                at = done + half + i
                ocean = mask_ref[order[at] : order[at] + 1, :].astype(f32)
                value = ((y[:, i * lanes : (i + 1) * lanes] + bias) * ocean).astype(bf16)
                f_ref[at] = value
                packed = pack_edges(packed, value, half + i)
        e_ref[done // 16] = packed
        done += size


def stem(state, weight_t, bias_wide, mask, order):
    d = weight_t.shape[0]
    n = len(order)
    groups = -(-n // 16)
    return pl.pallas_call(
        functools.partial(stem_body, order),
        out_shape=[
            jax.ShapeDtypeStruct((n, d, lanes), bf16),
            jax.ShapeDtypeStruct((groups, d, lanes), bf16),
        ],
        name="stem",
        **params_for(2 * d * state.size, 2 * state.size + 2 * n * d * lanes),
    )(state, weight_t, bias_wide, mask)


def band_body(segments, v_ref, o_ref):
    m, k = o_ref.shape[1:]
    width = v_ref.shape[1]
    row = lax.broadcasted_iota(jnp.int32, (m, width), 0)

    def step(g, _):
        for u in range(8):
            c = g * 8 + u
            spread = jnp.broadcast_to(v_ref[pl.ds(c, 1), :], (m, width))
            band = None
            for first, shift in segments:
                turned = pltpu.roll(spread, shift, 1, stride=1, stride_axis=0)
                band = turned if band is None else jnp.where(row < first, band, turned)
            o_ref[c] = band[:, :k].astype(bf16)
        return 0

    lax.fori_loop(0, v_ref.shape[0] // 8, step, 0)


def band(dw, window, m, segments):
    d = dw.shape[0]
    k = 7 * window
    width = -(-k // lanes) * lanes
    taps = jnp.transpose(dw, (0, 2, 1))
    taps = jnp.pad(taps, ((0, 0), (0, 0), (0, window - 7))).reshape(d, k)
    taps = jnp.pad(taps, ((0, 0), (0, width - k)))
    return pl.pallas_call(
        functools.partial(band_body, segments),
        out_shape=jax.ShapeDtypeStruct((d, m, k), bf16),
        name="bands",
        **params_for(0, 2 * d * m * k),
    )(taps)


def block_body(plan, head, *refs):
    feats = refs[: plan["sources"]]
    refs = refs[plan["sources"] :]
    (band_ref, dwb_ref, gain_ref, lnb_ref, w1_ref, w2_ref, ones_ref, ls_ref, lsb_ref, mask_ref) = refs[:10]
    refs = refs[10:]
    if head:
        head_ref = refs[0]
        refs = refs[1 + plan["carried"] :]
        out_ref, conv_ref, tend_ref, sems = refs
    else:
        f_ref, e_ref, conv_ref = refs
    window, out_rows = plan["window"], plan["out_rows"]
    p, m = len(window), len(out_rows)
    d = band_ref.shape[0]
    lane = lane_index((p, lanes))
    left_part = ((lane_index((16, lanes)) + 4) & 7) < 4

    def conv_step(g, _):
        cs = pl.ds(pl.multiple_of(g * 16, 16), 16)
        halos = {}
        xs, hs = [], []
        zero = jnp.zeros((16, lanes), bf16)
        for start in range(0, p, 16):
            xrow, hrow = [], []
            for entry in window[start : start + 16]:
                if entry is None:
                    xrow.append(zero)
                    hrow.append(zero)
                    continue
                src, at, left, right, slot = entry
                xrow.append(feats[src][at, cs, :])
                if (left, right) not in halos:
                    halos[left, right] = jnp.where(
                        left_part, feats[left[0]][left[1], cs, :], feats[right[0]][right[1], cs, :]
                    )
                both = halos[left, right]
                hrow.append(both if slot == 0 else pltpu.roll(both, lanes - 8 * slot, 1))
            xs.append(jnp.swapaxes(jnp.stack(xrow), 0, 1))
            hs.append(jnp.swapaxes(jnp.stack(hrow), 0, 1))
        for u in range(16):
            x = jnp.concatenate([part[u] for part in xs], axis=0)
            h = jnp.concatenate([part[u] for part in hs], axis=0)
            shifted = []
            for s in range(-3, 4):
                if s == 0:
                    shifted.append(x)
                    continue
                past = (lane < s) if s > 0 else (lane >= lanes + s)
                shifted.append(pltpu.roll(jnp.where(past, h, x), (-s) % lanes, 1))
            taps = jnp.concatenate(shifted, axis=0)
            conv_ref[g * 16 + u] = jnp.dot(band_ref[g * 16 + u], taps, preferred_element_type=f32)
        return 0

    lax.fori_loop(0, d // 16, conv_step, 0)

    packed = None
    for k in range(m // 8):
        y = conv_ref[:, 8 * k : 8 * k + 8, :] + dwb_ref[...]
        average = jnp.sum(y, axis=0, keepdims=True) * (1.0 / d)
        centered = y - average
        variance = jnp.sum(centered * centered, axis=0, keepdims=True) * (1.0 / d)
        normed = centered * lax.rsqrt(variance + ln_eps) * gain_ref[...] + lnb_ref[...]
        normed = jnp.swapaxes(normed, 0, 1).astype(bf16)
        joined = jnp.concatenate([normed[i] for i in range(8)], axis=1)
        joined = jnp.concatenate([joined, ones_ref[...]], axis=0)
        hidden = jnp.dot(w1_ref[...], joined, preferred_element_type=f32)
        hidden = (hidden + hidden * lax.erf(hidden * 0.7071067811865476)).astype(bf16)
        projected = jnp.dot(w2_ref[...], hidden, preferred_element_type=f32)
        updated = []
        for i in range(8):
            row = out_rows[8 * k + i]
            src, at = plan["residual"][8 * k + i]
            ocean = mask_ref[row : row + 1, :].astype(f32)
            branch = projected[:, i * lanes : (i + 1) * lanes] * ls_ref[...] + lsb_ref[...]
            value = ((feats[src][at].astype(f32) + branch) * ocean).astype(bf16)
            updated.append(value)
            if not head:
                f_ref[8 * k + i] = value
                slot = (8 * k + i) % 16
                packed = pack_edges(packed if slot else None, value, slot)
                if slot == 15:
                    e_ref[(8 * k + i) // 16] = packed
        if head:
            joined = jnp.concatenate(updated, axis=1)
            t = jnp.dot(head_ref[...], joined, preferred_element_type=f32)
            t = jnp.stack([t[:, i * lanes : (i + 1) * lanes] for i in range(8)])
            tend_ref[:, 8 * k : 8 * k + 8, :] = jnp.swapaxes(t, 0, 1)
            first = out_rows[8 * k]
            pltpu.make_async_copy(
                tend_ref.at[:, pl.ds(8 * k, 8), :], out_ref.at[:, pl.ds(first, 8), :], sems.at[k]
            ).start()
    if head:
        for k in range(m // 8):
            first = out_rows[8 * k]
            pltpu.make_async_copy(
                tend_ref.at[:, pl.ds(8 * k, 8), :], out_ref.at[:, pl.ds(first, 8), :], sems.at[k]
            ).wait()


def block(plan, feats, bands, layer, mask, head=None, carried=None):
    d = bands.shape[0]
    m = len(plan["out_rows"])
    hid = layer[3].shape[0]
    plan = dict(plan, sources=len(feats), carried=0 if carried is None else 1)
    flops = 2 * m * lanes * (2 * d * hid + d * 7 * len(plan["window"]))
    operands = [*feats, bands, *layer, mask]
    scratch = [pltpu.VMEM((d, m, lanes), f32)]
    if head is None:
        return pl.pallas_call(
            functools.partial(block_body, plan, False),
            out_shape=[
                jax.ShapeDtypeStruct((m, d, lanes), bf16),
                jax.ShapeDtypeStruct((m // 16, d, lanes), bf16),
            ],
            scratch_shapes=scratch,
            name="block",
            **params_for(flops, 20 * m * d * lanes),
        )(*operands)
    vmem = pl.BlockSpec(memory_space=pltpu.VMEM)
    anywhere = pl.BlockSpec(memory_space=pl.ANY)
    c_out = head.shape[0]
    specs = [vmem] * (len(operands) + 1)
    operands.append(head)
    aliases = {}
    if carried is not None:
        aliases = {len(operands): 0}
        operands.append(carried)
        specs.append(anywhere)
    scratch += [pltpu.VMEM((c_out, m, lanes), f32), pltpu.SemaphoreType.DMA((m // 8,))]
    return pl.pallas_call(
        functools.partial(block_body, plan, True),
        out_shape=jax.ShapeDtypeStruct((c_out, mask.shape[0], lanes), f32),
        in_specs=specs,
        out_specs=anywhere,
        scratch_shapes=scratch,
        input_output_aliases=aliases,
        name="block_head",
        **params_for(flops, 20 * m * d * lanes),
    )(*operands)


def filled(window):
    return window + [None] * (-len(window) % 16)


def body(
    q_state,
    scales,
    land_mask,
    stem_weight,
    stem_bias,
    dw_weight,
    dw_bias,
    ln_gain,
    ln_bias,
    w_in,
    b_in,
    w_out,
    b_out,
    layer_scale,
    head_weight,
):
    n_lat = lax.axis_size("lat")
    n_lon = lax.axis_size("lon")
    rows = land_mask.shape[0]
    d = stem_weight.shape[1]
    axes = ("lat", "lon")

    edge_send, mid_send = prep(q_state, scales, n_lat, n_lon, rows)

    def regroup(part):
        got = lax.all_to_all(part, axes, split_axis=0, concat_axis=0, tiled=True)
        return got.reshape(-1, part.shape[2], lanes)

    edge_state = regroup(edge_send)
    mid_state = regroup(mid_send)

    def wide(v):
        return jnp.broadcast_to(v[:, None], (v.shape[0], lanes))

    def wide8(v):
        return jnp.broadcast_to(v[:, None, None], (v.shape[0], 8, lanes))

    ones = jnp.broadcast_to(
        (lax.broadcasted_iota(jnp.int32, (16, 8 * lanes), 0) < 3).astype(bf16), (16, 8 * lanes)
    )

    def layer_of(b):
        high = b_in[b].astype(bf16)
        rest = b_in[b] - high.astype(f32)
        mid = rest.astype(bf16)
        low = (rest - mid.astype(f32)).astype(bf16)
        terms = jnp.stack([high, mid, low], axis=1)
        w1 = jnp.concatenate([w_in[b].T, jnp.pad(terms, ((0, 0), (0, 13)))], axis=1)
        return (
            wide8(dw_bias[b]),
            wide8(ln_gain[b]),
            wide8(ln_bias[b]),
            w1,
            w_out[b].T,
            ones,
            wide(layer_scale[b] * 0.5),
            wide(layer_scale[b] * b_out[b]),
        )

    layers = [layer_of(b) for b in range(2)]
    two = ((0, 0), (16, 6))
    bands_edge1 = band(dw_weight[0], 48, 32, two)
    bands_mid1 = band(dw_weight[0], 48, 32, ((0, 0),))
    bands_edge2 = band(dw_weight[1], 32, 16, ((0, 0), (8, 6)))
    bands_mid2 = band(dw_weight[1], 64, 48, ((0, 0),))

    def lon_exchange(packed):
        return (
            lax.ppermute(packed, "lon", [(i, (i + 1) % n_lon) for i in range(n_lon)]),
            lax.ppermute(packed, "lon", [((i + 1) % n_lon, i) for i in range(n_lon)]),
        )

    def lat_exchange(feat, left, right, first, last):
        def send(at, group):
            return jnp.concatenate(
                [feat[at : at + 3], left[group : group + 1], right[group : group + 1]], axis=0
            )

        north = lax.ppermute(send(*last), "lat", [(i, i + 1) for i in range(n_lat - 1)])
        south = lax.ppermute(send(*first), "lat", [(i + 1, i) for i in range(n_lat - 1)])
        return north, south

    weight_t = stem_weight.T
    stem_wide = wide(stem_bias)

    fe, ee = stem(edge_state, weight_t, stem_wide, land_mask, edge_order)
    el, er = lon_exchange(ee)
    north, south = lat_exchange(fe, el, er, (0, 0), (29, 1))

    def own(order, src, left, right):
        return {
            r: (src, t, (left, t // 16), (right, t // 16), t % 16) for t, r in enumerate(order)
        }

    def lat_halo(src_n, src_s, last_slot):
        got = {}
        for i in range(3):
            got[i - 3] = (src_n, i, (src_n, 3), (src_n, 4), last_slot + i)
            got[rows + i] = (src_s, i, (src_s, 3), (src_s, 4), i)
        return got

    def plan_of(table, groups):
        window, out_rows = [], []
        for first, last in groups:
            window += [table[r] for r in range(first - 3, last + 3)]
            out_rows += list(range(first, last))
        return dict(
            window=filled(window),
            out_rows=out_rows,
            residual=[table[r][:2] for r in out_rows],
        )

    table = {**own(edge_order, 0, 1, 2), **lat_halo(3, 4, 13)}
    edge1_order = [*range(0, 16), *range(48, 64)]
    ge, pe = block(
        plan_of(table, [(0, 16), (48, 64)]),
        (fe, el, er, north, south),
        bands_edge1,
        layers[0],
        land_mask,
    )

    fm, em = stem(mid_state, weight_t, stem_wide, land_mask, mid_order)
    ml, mr = lon_exchange(em)
    table = {**own(edge_order, 0, 1, 2), **own(mid_order, 3, 4, 5)}
    gm, pm = block(
        plan_of(table, [(16, 48)]),
        (fe, el, er, fm, ml, mr),
        bands_mid1,
        layers[0],
        land_mask,
    )

    gel, ger = lon_exchange(pe)
    gnorth, gsouth = lat_exchange(ge, gel, ger, (0, 0), (29, 1))
    gml, gmr = lon_exchange(pm)
    head_t = head_weight.T
    table = {**own(edge1_order, 0, 1, 2), **lat_halo(3, 4, 13)}
    out = block(
        plan_of(table, [(0, 8), (56, 64)]),
        (ge, gel, ger, gnorth, gsouth),
        bands_edge2,
        layers[1],
        land_mask,
        head=head_t,
    )
    table = {**own(edge1_order, 0, 1, 2), **own(range(16, 48), 3, 4, 5)}
    return block(
        plan_of(table, [(8, 56)]),
        (ge, gel, ger, gm, gml, gmr),
        bands_mid2,
        layers[1],
        land_mask,
        head=head_t,
        carried=out,
    )


def solution(mesh):
    placed = (
        P(("lat", "lon"), None, None),
        P(("lat", "lon"), None),
        P("lat", "lon"),
        *([P()] * 12),
    )
    return jax.shard_map(
        body, mesh=mesh, in_specs=placed, out_specs=P(None, "lat", "lon"), check_vma=False
    )
```

```python
import functools

import jax
import jax.numpy as jnp
import numpy as np
from jax import lax
from jax.experimental import pallas as pl
from jax.experimental.pallas import tpu as pltpu
from jax.sharding import PartitionSpec as P

ln_eps = 1e-06
f32 = jnp.float32
bf16 = jnp.bfloat16
lanes = 128
half = lanes // 2
mib = 2**20


halo_chunk = -1


def window_of(span):
    per = span // 16
    even, odd = list(range(per)), list(range(per, 2 * per))
    order = []
    for s in range(-2, 3):
        chunks = (even if s > -2 else []) + (odd if s < 2 else []) + [halo_chunk]
        order += [(s, c) for c in chunks]
    return order


def window_tables(span):
    per = span // 16
    cols, rows = [], []
    for s, c in window_of(span):
        if c == halo_chunk:
            for phase in range(2):
                cols += [2 * s + phase] * 8
                rows += [-3, -2, -1, span, span + 1, span + 2, 10000, 10000]
        else:
            cols += [2 * s + c // per] * 16
            rows += [16 * (c % per) + q for q in range(16)]
    return np.array([cols], np.int32), np.array([rows], np.int32)


def params_for(vmem, flops=0, bytes_accessed=0):
    return dict(
        compiler_params=pltpu.CompilerParams(vmem_limit_bytes=vmem * mib),
        cost_estimate=pl.CostEstimate(
            flops=int(flops), bytes_accessed=int(bytes_accessed), transcendentals=0
        ),
    )


def lane_index(shape):
    return lax.broadcasted_iota(jnp.int32, shape, len(shape) - 1)


def row_index(shape):
    return lax.broadcasted_iota(jnp.int32, shape, 0)


def turn(x, amount):
    amount %= lanes
    return pltpu.roll(x, amount, 1) if amount else x


def prep_body(q_ref, s_ref, o_ref):
    channels, rows, cols = q_ref.shape
    tiles = cols // lanes
    span = rows // 2
    shape = (lanes, 2 * lanes)
    to = lane_index(shape)
    at = to & (lanes - 1)
    phase = (at >> 6) ^ (to >> 7)
    order = (row_index(shape) == 2 * (at & (half - 1)) + phase).astype(f32).astype(bf16)
    left = lane_index((span, lanes)) < half
    for c in range(channels):
        scale = jnp.broadcast_to(s_ref[:, c : c + 1], (rows, lanes))
        x = jnp.concatenate(
            [
                (q_ref[c, :, b * lanes : (b + 1) * lanes].astype(f32) * scale).astype(bf16)
                for b in range(tiles)
            ],
            axis=0,
        )
        y = jnp.dot(x, order, preferred_element_type=f32)
        for b in range(tiles):
            top = y[b * rows : b * rows + span]
            low = y[b * rows + span : (b + 1) * rows]
            o_ref[0, b, c, 0:span] = jnp.where(left, top[:, :lanes], low[:, lanes:]).astype(bf16)
            o_ref[0, b, c, span:rows] = jnp.where(left, top[:, lanes:], low[:, :lanes]).astype(bf16)


def prep(q_state, scales, n_lat, n_lon, rows):
    channels, n_rows, n_cols = q_state.shape
    return pl.pallas_call(
        prep_body,
        grid=(n_lat,),
        in_specs=[
            pl.BlockSpec((channels, rows, n_cols), lambda a: (0, a, 0)),
            pl.BlockSpec((rows, channels), lambda a: (a, 0)),
        ],
        out_specs=pl.BlockSpec((1, n_lon, channels, rows, lanes), lambda a: (a, 0, 0, 0, 0)),
        out_shape=jax.ShapeDtypeStruct((n_lat, n_lon, channels, rows, lanes), bf16),
        name="dequantize",
        **params_for(20, 0, 4 * q_state.size),
    )(q_state, scales.T).reshape(n_lat * n_lon, channels, rows, lanes)


def slot_of(shape):
    return ((lane_index(shape) + 2) >> 2) & 15


def pack_edges(packed, lead, slot):
    turned = turn(lead, 4 * slot)
    return jnp.where(slot_of(lead.shape) == slot, turned, packed)


def first_ends(shape):
    return ((lane_index(shape) + 2) & 3) >= 2


def messages(f_ref, e_ref, west_ref, east_ref, south_ref, north_ref):
    shape = f_ref.shape[1:]
    span = f_ref.shape[0] // 2
    first = first_ends(shape)
    for i in range(e_ref.shape[0] // 2):
        one, two = e_ref[2 * i], e_ref[2 * i + 1]
        west_ref[i] = jnp.where(first, one, turn(two, -2))
        east_ref[i] = jnp.where(first, turn(two, 2), one)
    left = lane_index(shape) < half
    for i in range(3):
        r = span - 3 + i
        south_ref[i] = jnp.where(left, turn(f_ref[r], half), f_ref[span + r])
        north_ref[i] = jnp.where(left, f_ref[i], turn(f_ref[span + i], half))


def received_ends(from_west, from_east):
    first = first_ends(from_west[0].shape)
    groups = []
    for west, east in zip(from_west, from_east):
        groups.append(jnp.where(first, east, west))
        groups.append(jnp.where(first, turn(east, 2), turn(west, -2)))
    return groups


def rows_body(west_in, east_in, south_in, north_in, south_ref, north_ref):
    count = west_in.shape[0]
    groups = received_ends([west_in[i] for i in range(count)], [east_in[i] for i in range(count)])
    slot = slot_of(groups[0].shape)
    south_ref[0:3] = south_in[...]
    north_ref[0:3] = north_in[...]
    south_ref[3] = jnp.where(slot > 11, groups[count - 1], turn(groups[2 * count - 1], -32))
    north_ref[3] = jnp.where(slot < 4, groups[0], turn(groups[count], 32))


def rows_with_ends(from_west, from_east, to_south, to_north):
    shape = jax.ShapeDtypeStruct((4, *to_south.shape[1:]), bf16)
    return pl.pallas_call(
        rows_body,
        out_shape=[shape, shape],
        name="rows",
        **params_for(20, 0, 20 * to_south.size),
    )(from_west, from_east, to_south, to_north)


def stem_body(x_ref, w_ref, wide_ref, mask_ref, f_ref, west_ref, east_ref, south_ref, north_ref, e_ref):
    bias = wide_ref[4]
    for g in range(x_ref.shape[1] // 16):
        x = jnp.swapaxes(x_ref[:, 16 * g : 16 * g + 16, :], 0, 1)
        packed = jnp.zeros(f_ref.shape[1:], bf16)
        for first in (0, 8):
            joined = jnp.concatenate([x[first + i] for i in range(8)], axis=1)
            y = jnp.dot(w_ref[...], joined, preferred_element_type=f32)
            for i in range(8):
                at = 16 * g + first + i
                value = (y[:, i * lanes : (i + 1) * lanes] + bias) * mask_ref[at : at + 1, :]
                value = value.astype(bf16)
                f_ref[at] = value
                packed = pack_edges(packed, value, first + i)
        e_ref[g] = packed
    messages(f_ref, e_ref, west_ref, east_ref, south_ref, north_ref)


def feature_shapes(leads, d):
    return [
        jax.ShapeDtypeStruct((n, d, lanes), bf16) for n in (leads, leads // 32, leads // 32, 3, 3)
    ]


def stem(state, weight_t, wide, mask):
    d = weight_t.shape[0]
    leads = state.shape[1]
    return pl.pallas_call(
        stem_body,
        out_shape=feature_shapes(leads, d),
        scratch_shapes=[pltpu.VMEM((leads // 16, d, lanes), bf16)],
        name="stem",
        **params_for(20, 2 * d * state.size, 2 * state.size + 2 * leads * d * lanes),
    )(state, weight_t, wide, mask)


def band_body(w_ref, col_ref, row_ref, o_ref):
    k = o_ref.shape[2]
    taps = w_ref.shape[1]
    at = row_index((taps, k))
    made = []
    for q in range(16):
        i = row_ref[...] - (8 * pl.program_id(0) + q % 8) + 3
        j = col_ref[...] - q // 8 + 3
        tap = jnp.where((i >= 0) & (i < 7) & (j >= 0) & (j < 7), 7 * i + j, -1)
        pick = (at == tap).astype(f32).astype(bf16)
        made.append(jnp.dot(w_ref[...], pick, preferred_element_type=f32).astype(bf16))
    o_ref[...] = jnp.swapaxes(jnp.stack(made), 0, 1)


def band(dw, span):
    d = dw.shape[0]
    cols, rows = window_tables(span)
    k = cols.shape[1]
    taps = jnp.pad(dw.reshape(d, 49), ((0, 0), (0, 15))).astype(bf16)
    return pl.pallas_call(
        band_body,
        grid=(span // 8,),
        in_specs=[
            pl.BlockSpec((d, 64), lambda u: (0, 0)),
            pl.BlockSpec((1, k), lambda u: (0, 0)),
            pl.BlockSpec((1, k), lambda u: (0, 0)),
        ],
        out_specs=pl.BlockSpec((d, 16, k), lambda u: (0, u, 0)),
        out_shape=jax.ShapeDtypeStruct((d, 2 * span, k), bf16),
        name="bands",
        **params_for(20, 0, 4 * d * span * k),
    )(taps, jnp.asarray(cols), jnp.asarray(rows))


def block_body(index, head, *refs):
    f_in, west_in, east_in, north_in, south_in, band_ref = refs[:6]
    thin_ref, wide_ref, w1_ref, w2_ref, mask_ref, edge_ref = refs[6:12]
    refs = refs[12:]
    if head:
        head_ref, out_ref, conv_ref, held_ref, band_sems, tend_ref, sems = refs
    else:
        f_ref, *sent_refs, conv_ref, held_ref, band_sems, e_ref = refs
    leads, d = f_in.shape[:2]
    span = leads // 2
    per = span // 16

    def fetch(g):
        cs = pl.ds(g * 16, 16)
        return pltpu.make_async_copy(band_ref.at[cs], held_ref.at[cs], band_sems.at[g])

    for g in range(d // 16):
        fetch(g).start()

    small = (16, lanes)
    left = lane_index(small) < half
    place = lane_index(small) & (half - 1)

    def conv_step(g, _):
        cs = pl.ds(pl.multiple_of(g * 16, 16), 16)
        fetch(g).wait()
        zero = jnp.zeros(small, bf16)

        def ends(group, slot):
            return turn(group, half - 4 * slot)

        count = leads // 32
        packs = received_ends(
            [west_in[i, cs, :] for i in range(count)], [east_in[i, cs, :] for i in range(count)]
        )
        norths = [north_in[i, cs, :] * edge_ref[0] for i in range(4)]
        souths = [south_in[i, cs, :] * edge_ref[1] for i in range(4)]
        chunks = {}
        for k in range(leads // 16):
            x = jnp.stack([f_in[16 * k + q, cs, :] for q in range(16)])
            h = jnp.stack([ends(packs[k], q) for q in range(16)])
            chunks[k] = (jnp.swapaxes(x, 0, 1), jnp.swapaxes(h, 0, 1))
        xrow, hrow = [], []
        for phase in range(2):
            for i in range(3):
                r = span - 3 + i
                own = f_in[phase * span + r, cs, :]
                got = norths[i]
                if phase == 0:
                    xrow.append(jnp.where(left, got, turn(own, half)))
                else:
                    xrow.append(turn(jnp.where(left, own, got), half))
                slot = r % 16
                mine = ends(packs[phase * per + r // 16], slot)
                theirs = ends(norths[3], slot - 8 * phase)
                hrow.append(turn(jnp.where(left, theirs, mine), half))
            for i in range(3):
                own = f_in[phase * span + i, cs, :]
                got = souths[i]
                if phase == 0:
                    xrow.append(turn(jnp.where(left, got, own), half))
                else:
                    xrow.append(jnp.where(left, turn(own, half), got))
                mine = ends(packs[phase * per], i)
                theirs = ends(souths[3], i + 8 * phase)
                hrow.append(turn(jnp.where(left, mine, theirs), half))
            xrow += [zero, zero]
            hrow += [zero, zero]
        chunks[halo_chunk] = tuple(jnp.swapaxes(jnp.stack(v), 0, 1) for v in (xrow, hrow))
        for u in range(16):
            taps = []
            for s, c in window_of(span):
                x, h = chunks[c][0][u], chunks[c][1][u]
                if s:
                    past = (place < s) if s > 0 else (place >= half + s)
                    x = turn(jnp.where(past, h, x), -s)
                taps.append(x)
            taps = jnp.concatenate(taps, axis=0)
            conv_ref[g * 16 + u] = jnp.dot(held_ref[g * 16 + u], taps, preferred_element_type=f32)
        return 0

    lax.fori_loop(0, d // 16, conv_step, 0)

    if head:
        shape = (2 * lanes, 2 * lanes)
        to, at = lane_index(shape), row_index(shape)
        col = to & (lanes - 1)
        source = (col & 1) * lanes + (to >> 7) * half + (col >> 1)
        back = (at == source).astype(f32).astype(bf16)
    ones = (row_index((16, 8 * lanes)) < 3).astype(f32).astype(bf16)
    dwb, gain, lnb = (thin_ref.at[3 * index + i] for i in range(3))
    ls, lsb = wide_ref[2 * index], wide_ref[2 * index + 1]
    held = []
    for k in range(leads // 8):
        u, phase = k // 2, k % 2
        lead = phase * span + 8 * u
        y = conv_ref[:, 8 * k : 8 * k + 8, :] + dwb[...]
        average = jnp.sum(y, axis=0, keepdims=True) * (1.0 / d)
        centered = y - average
        variance = jnp.sum(centered * centered, axis=0, keepdims=True) * (1.0 / d)
        normed = centered * lax.rsqrt(variance + ln_eps) * gain[...] + lnb[...]
        normed = jnp.swapaxes(normed, 0, 1).astype(bf16)
        joined = jnp.concatenate([normed[i] for i in range(8)], axis=1)
        joined = jnp.concatenate([joined, ones], axis=0)
        hidden = jnp.dot(w1_ref[...], joined, preferred_element_type=f32)
        hidden = (hidden + hidden * lax.erf(hidden * 0.7071067811865476)).astype(bf16)
        projected = jnp.dot(w2_ref[...], hidden, preferred_element_type=f32)
        if not head:
            packed = jnp.zeros((d, lanes), bf16) if lead % 16 == 0 else e_ref[lead // 16]
        for i in range(8):
            ocean = mask_ref[lead + i : lead + i + 1, :]
            branch = projected[:, i * lanes : (i + 1) * lanes] * ls + lsb
            value = ((f_in[lead + i].astype(f32) + branch) * ocean).astype(bf16)
            if head:
                held.append(value)
            else:
                f_ref[lead + i] = value
                packed = pack_edges(packed, value, (lead + i) % 16)
        if not head:
            e_ref[lead // 16] = packed
        elif phase == 1:
            both = [jnp.concatenate([held[i], held[8 + i]], axis=1) for i in range(8)]
            both = jnp.dot(jnp.concatenate(both, axis=0), back, preferred_element_type=f32)
            both = both.astype(bf16)
            for part in range(2):
                cut = slice(part * lanes, (part + 1) * lanes)
                joined = jnp.concatenate([both[i * d : (i + 1) * d, cut] for i in range(8)], axis=1)
                t = jnp.dot(head_ref[...], joined, preferred_element_type=f32)
                t = jnp.stack([t[:, i * lanes : (i + 1) * lanes] for i in range(8)])
                at = part * span + 8 * u
                tend_ref[:, at : at + 8, :] = jnp.swapaxes(t, 0, 1)
                cut = pl.ds(at, 8)
                pltpu.make_async_copy(
                    tend_ref.at[:, cut, :], out_ref.at[:, cut, :], sems.at[at // 8]
                ).start()
            held = []
    if head:
        for at in range(0, leads, 8):
            cut = pl.ds(at, 8)
            pltpu.make_async_copy(
                tend_ref.at[:, cut, :], out_ref.at[:, cut, :], sems.at[at // 8]
            ).wait()
    else:
        messages(f_ref, e_ref, *sent_refs)


def block(index, feats, bands, params, head=None):
    d, leads, k = bands.shape
    hid = params[2].shape[0]
    flops = 2 * leads * lanes * (2 * d * hid + d * k)
    operands = [*feats, bands, *params]
    vmem = pl.BlockSpec(memory_space=pltpu.VMEM)
    anywhere = pl.BlockSpec(memory_space=pl.ANY)
    specs = [vmem] * len(feats) + [anywhere] + [vmem] * len(params)
    scratch = [
        pltpu.VMEM((d, leads, lanes), f32),
        pltpu.VMEM(bands.shape, bf16),
        pltpu.SemaphoreType.DMA((d // 16,)),
    ]
    if head is None:
        return pl.pallas_call(
            functools.partial(block_body, index, False),
            out_shape=feature_shapes(leads, d),
            in_specs=specs,
            scratch_shapes=scratch + [pltpu.VMEM((leads // 16, d, lanes), bf16)],
            name="block",
            **params_for(44, flops, 20 * leads * d * lanes),
        )(*operands)
    c_out = head.shape[0]
    scratch += [pltpu.VMEM((c_out, leads, lanes), f32), pltpu.SemaphoreType.DMA((leads // 8,))]
    return pl.pallas_call(
        functools.partial(block_body, index, True),
        out_shape=jax.ShapeDtypeStruct((c_out, leads, lanes), f32),
        in_specs=specs + [vmem],
        out_specs=anywhere,
        scratch_shapes=scratch,
        name="block_head",
        **params_for(44, flops, 20 * leads * d * lanes),
    )(*operands, head)


def body(
    q_state,
    scales,
    land_mask,
    stem_weight,
    stem_bias,
    dw_weight,
    dw_bias,
    ln_gain,
    ln_bias,
    w_in,
    b_in,
    w_out,
    b_out,
    layer_scale,
    head_weight,
):
    n_lat = lax.axis_size("lat")
    n_lon = lax.axis_size("lon")
    rows = land_mask.shape[0]
    span = rows // 2
    axes = ("lat", "lon")

    send = prep(q_state, scales, n_lat, n_lon, rows)
    state = lax.all_to_all(send, axes, split_axis=0, concat_axis=0, tiled=True)
    state = state.reshape(-1, rows, lanes)

    mask = land_mask.astype(f32).reshape(2, span, half, 2).transpose(3, 1, 0, 2)
    mask = mask.reshape(rows, lanes)
    d = stem_weight.shape[1]
    thin = jnp.stack([dw_bias, ln_gain, ln_bias], axis=1).reshape(6, d)
    thin = jnp.broadcast_to(thin[:, :, None, None], (6, d, 1, lanes))
    wide = jnp.stack([layer_scale * 0.5, layer_scale * b_out], axis=1).reshape(4, d)
    wide = jnp.concatenate([wide, stem_bias[None]], axis=0)
    wide = jnp.broadcast_to(wide[:, :, None], (5, d, lanes))
    high = b_in.astype(bf16)
    rest = b_in - high.astype(f32)
    mid = rest.astype(bf16)
    low = (rest - mid.astype(f32)).astype(bf16)
    terms = jnp.pad(jnp.stack([high, mid, low], axis=2), ((0, 0), (0, 0), (0, 13)))
    w1 = jnp.concatenate([w_in.transpose(0, 2, 1), terms], axis=2)
    w2 = w_out.transpose(0, 2, 1)
    band_at = lax.axis_index("lat")
    edge = jnp.stack([band_at > 0, band_at < n_lat - 1]).astype(bf16)
    edge = jnp.broadcast_to(edge[:, None, None], (2, 16, lanes))
    dw_weight, ready = lax.optimization_barrier(
        (dw_weight, (thin, wide, w1, w2, stem_weight.T, mask, edge, head_weight.T))
    )
    bands = [band(dw_weight[b], span) for b in range(2)]
    state, bands, (thin, wide, w1, w2, weight_t, mask, edge, head_t) = lax.optimization_barrier(
        (state, bands, ready)
    )

    def shift(x, axis, by):
        n = lax.axis_size(axis)
        return lax.ppermute(x, axis, [(i, (i + by) % n) for i in range(n)])

    def exchange(feat, to_west, to_east, to_south, to_north):
        from_west, from_east = shift(to_east, "lon", 1), shift(to_west, "lon", -1)
        to_south, to_north = rows_with_ends(from_west, from_east, to_south, to_north)
        return feat, from_west, from_east, shift(to_south, "lat", 1), shift(to_north, "lat", -1)

    feats = stem(state, weight_t, wide, mask)
    feats = block(0, exchange(*feats), bands[0], (thin, wide, w1[0], w2[0], mask, edge))
    return block(1, exchange(*feats), bands[1], (thin, wide, w1[1], w2[1], mask, edge), head_t)


def solution(mesh):
    placed = (
        P(("lat", "lon"), None, None),
        P(("lat", "lon"), None),
        P("lat", "lon"),
        *([P()] * 12),
    )
    return jax.shard_map(
        body, mesh=mesh, in_specs=placed, out_specs=P(None, "lat", "lon"), check_vma=False
    )
```

```python
import functools

import jax
import jax.numpy as jnp
import numpy as np
from jax import lax
from jax.experimental import pallas as pl
from jax.experimental.pallas import tpu as pltpu
from jax.sharding import PartitionSpec as P

ln_eps = 1e-06
f32 = jnp.float32
bf16 = jnp.bfloat16
lanes = 128
half = lanes // 2
mib = 2**20


halo_chunk = -1


def window_of(span):
    per = span // 16
    even, odd = list(range(per)), list(range(per, 2 * per))
    order = []
    for s in range(-2, 3):
        chunks = (even if s > -2 else []) + (odd if s < 2 else []) + [halo_chunk]
        order += [(s, c) for c in chunks]
    return order


def window_tables(span):
    per = span // 16
    cols, rows = [], []
    for s, c in window_of(span):
        if c == halo_chunk:
            for phase in range(2):
                cols += [2 * s + phase] * 8
                rows += [-3, -2, -1, span, span + 1, span + 2, 10000, 10000]
        else:
            cols += [2 * s + c // per] * 16
            rows += [16 * (c % per) + q for q in range(16)]
    return np.array([cols], np.int32), np.array([rows], np.int32)


def params_for(vmem, flops=0, bytes_accessed=0):
    return dict(
        compiler_params=pltpu.CompilerParams(vmem_limit_bytes=vmem * mib),
        cost_estimate=pl.CostEstimate(
            flops=int(flops), bytes_accessed=int(bytes_accessed), transcendentals=0
        ),
    )


def lane_index(shape):
    return lax.broadcasted_iota(jnp.int32, shape, len(shape) - 1)


def row_index(shape):
    return lax.broadcasted_iota(jnp.int32, shape, 0)


def turn(x, amount):
    amount %= lanes
    return pltpu.roll(x, amount, 1) if amount else x


def prep_body(q_ref, s_ref, o_ref):
    channels, rows, cols = q_ref.shape
    tiles = cols // lanes
    span = rows // 2
    shape = (lanes, 2 * lanes)
    to = lane_index(shape)
    at = to & (lanes - 1)
    phase = (at >> 6) ^ (to >> 7)
    order = (row_index(shape) == 2 * (at & (half - 1)) + phase).astype(f32).astype(bf16)
    left = lane_index((span, lanes)) < half
    every = (rows, s_ref.shape[1])
    for c in range(channels):
        own = lane_index(every) == row_index(every) + pl.program_id(0) * rows
        scale = jnp.sum(jnp.where(own, s_ref[c : c + 1, :], 0.0), axis=1, keepdims=True)
        x = jnp.concatenate(
            [
                (q_ref[c, :, b * lanes : (b + 1) * lanes].astype(f32) * scale).astype(bf16)
                for b in range(tiles)
            ],
            axis=0,
        )
        y = jnp.dot(x, order, preferred_element_type=f32)
        for b in range(tiles):
            top = y[b * rows : b * rows + span]
            low = y[b * rows + span : (b + 1) * rows]
            o_ref[0, b, c, 0:span] = jnp.where(left, top[:, :lanes], low[:, lanes:]).astype(bf16)
            o_ref[0, b, c, span:rows] = jnp.where(left, top[:, lanes:], low[:, :lanes]).astype(bf16)


def prep(q_state, scales, n_lat, n_lon, rows):
    channels, n_rows, n_cols = q_state.shape
    return pl.pallas_call(
        prep_body,
        grid=(n_lat,),
        in_specs=[
            pl.BlockSpec((channels, rows, n_cols), lambda a: (0, a, 0)),
            pl.BlockSpec((channels, n_rows), lambda a: (0, 0)),
        ],
        out_specs=pl.BlockSpec((1, n_lon, channels, rows, lanes), lambda a: (a, 0, 0, 0, 0)),
        out_shape=jax.ShapeDtypeStruct((n_lat, n_lon, channels, rows, lanes), bf16),
        name="dequantize",
        **params_for(60, 0, 4 * q_state.size),
    )(q_state, scales).reshape(n_lat * n_lon, channels, rows, lanes)


def slot_of(shape):
    return ((lane_index(shape) + 2) >> 2) & 15


def pack_edges(packed, lead, slot):
    turned = turn(lead, 4 * slot)
    return jnp.where(slot_of(lead.shape) == slot, turned, packed)


def first_ends(shape):
    return ((lane_index(shape) + 2) & 3) >= 2


def messages(f_ref, e_ref, west_ref, east_ref, south_ref, north_ref):
    shape = f_ref.shape[1:]
    span = f_ref.shape[0] // 2
    first = first_ends(shape)
    for i in range(e_ref.shape[0] // 2):
        one, two = e_ref[2 * i], e_ref[2 * i + 1]
        west_ref[i] = jnp.where(first, one, turn(two, -2))
        east_ref[i] = jnp.where(first, turn(two, 2), one)
    left = lane_index(shape) < half
    for i in range(3):
        r = span - 3 + i
        south_ref[i] = jnp.where(left, turn(f_ref[r], half), f_ref[span + r])
        north_ref[i] = jnp.where(left, f_ref[i], turn(f_ref[span + i], half))


def received_ends(from_west, from_east):
    first = first_ends(from_west[0].shape)
    groups = []
    for west, east in zip(from_west, from_east):
        groups.append(jnp.where(first, east, west))
        groups.append(jnp.where(first, turn(east, 2), turn(west, -2)))
    return groups


def rows_body(west_in, east_in, south_in, north_in, south_ref, north_ref):
    count = west_in.shape[0]
    groups = received_ends([west_in[i] for i in range(count)], [east_in[i] for i in range(count)])
    slot = slot_of(groups[0].shape)
    south_ref[0:3] = south_in[...]
    north_ref[0:3] = north_in[...]
    south_ref[3] = jnp.where(slot > 11, groups[count - 1], turn(groups[2 * count - 1], -32))
    north_ref[3] = jnp.where(slot < 4, groups[0], turn(groups[count], 32))


def rows_with_ends(from_west, from_east, to_south, to_north):
    shape = jax.ShapeDtypeStruct((4, *to_south.shape[1:]), bf16)
    return pl.pallas_call(
        rows_body,
        out_shape=[shape, shape],
        name="rows",
        **params_for(20, 0, 20 * to_south.size),
    )(from_west, from_east, to_south, to_north)


def stem_body(x_ref, w_ref, wide_ref, mask_ref, f_ref, west_ref, east_ref, south_ref, north_ref, e_ref):
    bias = wide_ref[4]
    for g in range(x_ref.shape[1] // 16):
        x = jnp.swapaxes(x_ref[:, 16 * g : 16 * g + 16, :], 0, 1)
        packed = jnp.zeros(f_ref.shape[1:], bf16)
        for first in (0, 8):
            joined = jnp.concatenate([x[first + i] for i in range(8)], axis=1)
            y = jnp.dot(w_ref[...], joined, preferred_element_type=f32)
            for i in range(8):
                at = 16 * g + first + i
                value = (y[:, i * lanes : (i + 1) * lanes] + bias) * mask_ref[at : at + 1, :]
                value = value.astype(bf16)
                f_ref[at] = value
                packed = pack_edges(packed, value, first + i)
        e_ref[g] = packed
    messages(f_ref, e_ref, west_ref, east_ref, south_ref, north_ref)


def feature_shapes(leads, d):
    return [
        jax.ShapeDtypeStruct((n, d, lanes), bf16) for n in (leads, leads // 32, leads // 32, 3, 3)
    ]


def stem(state, weight_t, wide, mask):
    d = weight_t.shape[0]
    leads = state.shape[1]
    return pl.pallas_call(
        stem_body,
        out_shape=feature_shapes(leads, d),
        scratch_shapes=[pltpu.VMEM((leads // 16, d, lanes), bf16)],
        name="stem",
        **params_for(20, 2 * d * state.size, 2 * state.size + 2 * leads * d * lanes),
    )(state, weight_t, wide, mask)


def band_body(w_ref, col_ref, row_ref, o_ref):
    k = o_ref.shape[2]
    taps = w_ref.shape[1]
    at = row_index((taps, k))
    made = []
    for q in range(16):
        i = row_ref[...] - (8 * pl.program_id(0) + q % 8) + 3
        j = col_ref[...] - q // 8 + 3
        tap = jnp.where((i >= 0) & (i < 7) & (j >= 0) & (j < 7), 7 * i + j, -1)
        pick = (at == tap).astype(f32).astype(bf16)
        made.append(jnp.dot(w_ref[...], pick, preferred_element_type=f32).astype(bf16))
    o_ref[...] = jnp.swapaxes(jnp.stack(made), 0, 1)


def band(dw, span):
    d = dw.shape[0]
    cols, rows = window_tables(span)
    k = cols.shape[1]
    taps = jnp.pad(dw.reshape(d, 49), ((0, 0), (0, 15))).astype(bf16)
    return pl.pallas_call(
        band_body,
        grid=(span // 8,),
        in_specs=[
            pl.BlockSpec((d, 64), lambda u: (0, 0)),
            pl.BlockSpec((1, k), lambda u: (0, 0)),
            pl.BlockSpec((1, k), lambda u: (0, 0)),
        ],
        out_specs=pl.BlockSpec((d, 16, k), lambda u: (0, u, 0)),
        out_shape=jax.ShapeDtypeStruct((d, 2 * span, k), bf16),
        name="bands",
        **params_for(20, 0, 4 * d * span * k),
    )(taps, jnp.asarray(cols), jnp.asarray(rows))


def block_body(index, head, *refs):
    f_in, west_in, east_in, north_in, south_in, band_ref = refs[:6]
    thin_ref, wide_ref, w1_ref, w2_ref, mask_ref, edge_ref = refs[6:12]
    refs = refs[12:]
    if head:
        head_ref, out_ref, conv_ref, held_ref, band_sems, sum_ref, tend_ref, sems = refs
    else:
        f_ref, *sent_refs, conv_ref, held_ref, band_sems, sum_ref, e_ref = refs
    leads, d = f_in.shape[:2]
    span = leads // 2
    per = span // 16

    def fetch(g):
        cs = pl.ds(g * 16, 16)
        return pltpu.make_async_copy(band_ref.at[cs], held_ref.at[cs], band_sems.at[g])

    for g in range(d // 16):
        fetch(g).start()

    small = (16, lanes)
    left = lane_index(small) < half
    place = lane_index(small) & (half - 1)

    def conv_step(g, _):
        cs = pl.ds(pl.multiple_of(g * 16, 16), 16)
        fetch(g).wait()
        zero = jnp.zeros(small, bf16)

        def ends(group, slot):
            return turn(group, half - 4 * slot)

        count = leads // 32
        packs = received_ends(
            [west_in[i, cs, :] for i in range(count)], [east_in[i, cs, :] for i in range(count)]
        )
        norths = [north_in[i, cs, :] * edge_ref[0] for i in range(4)]
        souths = [south_in[i, cs, :] * edge_ref[1] for i in range(4)]
        chunks = {}
        for k in range(leads // 16):
            x = jnp.stack([f_in[16 * k + q, cs, :] for q in range(16)])
            h = jnp.stack([ends(packs[k], q) for q in range(16)])
            chunks[k] = (jnp.swapaxes(x, 0, 1), jnp.swapaxes(h, 0, 1))
        xrow, hrow = [], []
        for phase in range(2):
            for i in range(3):
                r = span - 3 + i
                own = f_in[phase * span + r, cs, :]
                got = norths[i]
                if phase == 0:
                    xrow.append(jnp.where(left, got, turn(own, half)))
                else:
                    xrow.append(turn(jnp.where(left, own, got), half))
                slot = r % 16
                mine = ends(packs[phase * per + r // 16], slot)
                theirs = ends(norths[3], slot - 8 * phase)
                hrow.append(turn(jnp.where(left, theirs, mine), half))
            for i in range(3):
                own = f_in[phase * span + i, cs, :]
                got = souths[i]
                if phase == 0:
                    xrow.append(turn(jnp.where(left, got, own), half))
                else:
                    xrow.append(jnp.where(left, turn(own, half), got))
                mine = ends(packs[phase * per], i)
                theirs = ends(souths[3], i + 8 * phase)
                hrow.append(turn(jnp.where(left, mine, theirs), half))
            xrow += [zero, zero]
            hrow += [zero, zero]
        chunks[halo_chunk] = tuple(jnp.swapaxes(jnp.stack(v), 0, 1) for v in (xrow, hrow))
        total = squares = 0.0
        for u in range(16):
            taps = []
            for s, c in window_of(span):
                x, h = chunks[c][0][u], chunks[c][1][u]
                if s:
                    past = (place < s) if s > 0 else (place >= half + s)
                    x = turn(jnp.where(past, h, x), -s)
                taps.append(x)
            taps = jnp.concatenate(taps, axis=0)
            y = jnp.dot(held_ref[g * 16 + u], taps, preferred_element_type=f32)
            y = y + dwb[g * 16 + u]
            conv_ref[g * 16 + u] = y
            if u == 0:
                origin = conv_ref[0]
            y = y - origin
            total = total + y
            squares = squares + y * y
        sum_ref[0] += total
        sum_ref[1] += squares
        return 0

    dwb, gain, lnb = (thin_ref.at[3 * index + i] for i in range(3))
    sum_ref[...] = jnp.zeros_like(sum_ref)

    lax.fori_loop(0, d // 16, conv_step, 0)

    if head:
        shape = (2 * lanes, 2 * lanes)
        to, at = lane_index(shape), row_index(shape)
        col = to & (lanes - 1)
        source = (col & 1) * lanes + (to >> 7) * half + (col >> 1)
        back = (at == source).astype(f32).astype(bf16)
    ones = (row_index((16, 8 * lanes)) < 3).astype(f32).astype(bf16)
    ls, lsb = wide_ref[2 * index], wide_ref[2 * index + 1]
    held = []
    for k in range(leads // 8):
        u, phase = k // 2, k % 2
        lead = phase * span + 8 * u
        if phase == 0:
            cut = slice(8 * k, 8 * k + 16)
            average = sum_ref[0, cut, :] * (1.0 / d)
            variance = sum_ref[1, cut, :] * (1.0 / d) - average * average
            scale = lax.rsqrt(jnp.maximum(variance, 0.0) + ln_eps)
            centered = conv_ref[:, cut, :] - (conv_ref[0, cut, :] + average)
            both_normed = (centered * scale * gain[...] + lnb[...]).astype(bf16)
            both_normed = jnp.swapaxes(both_normed, 0, 1)
        normed = both_normed[8 * phase : 8 * phase + 8]
        joined = jnp.concatenate([normed[i] for i in range(8)], axis=1)
        joined = jnp.concatenate([joined, ones], axis=0)
        hidden = jnp.dot(w1_ref[...], joined, preferred_element_type=f32)
        hidden = (hidden + hidden * lax.erf(hidden * 0.7071067811865476)).astype(bf16)
        projected = jnp.dot(w2_ref[...], hidden, preferred_element_type=f32)
        if not head:
            packed = jnp.zeros((d, lanes), bf16) if lead % 16 == 0 else e_ref[lead // 16]
        for i in range(8):
            ocean = mask_ref[lead + i : lead + i + 1, :]
            branch = projected[:, i * lanes : (i + 1) * lanes] * ls + lsb
            value = ((f_in[lead + i].astype(f32) + branch) * ocean).astype(bf16)
            if head:
                held.append(value)
            else:
                f_ref[lead + i] = value
                packed = pack_edges(packed, value, (lead + i) % 16)
        if not head:
            e_ref[lead // 16] = packed
        elif phase == 1:
            both = [jnp.concatenate([held[i], held[8 + i]], axis=1) for i in range(8)]
            both = jnp.dot(jnp.concatenate(both, axis=0), back, preferred_element_type=f32)
            both = both.astype(bf16)
            for part in range(2):
                cut = slice(part * lanes, (part + 1) * lanes)
                joined = jnp.concatenate([both[i * d : (i + 1) * d, cut] for i in range(8)], axis=1)
                t = jnp.dot(head_ref[...], joined, preferred_element_type=f32)
                t = jnp.stack([t[:, i * lanes : (i + 1) * lanes] for i in range(8)])
                at = part * span + 8 * u
                tend_ref[:, at : at + 8, :] = jnp.swapaxes(t, 0, 1)
                cut = pl.ds(at, 8)
                pltpu.make_async_copy(
                    tend_ref.at[:, cut, :], out_ref.at[:, cut, :], sems.at[at // 8]
                ).start()
            held = []
    if head:
        for at in range(0, leads, 8):
            cut = pl.ds(at, 8)
            pltpu.make_async_copy(
                tend_ref.at[:, cut, :], out_ref.at[:, cut, :], sems.at[at // 8]
            ).wait()
    else:
        messages(f_ref, e_ref, *sent_refs)


def block(index, feats, bands, params, head=None):
    d, leads, k = bands.shape
    hid = params[2].shape[0]
    flops = 2 * leads * lanes * (2 * d * hid + d * k)
    operands = [*feats, bands, *params]
    vmem = pl.BlockSpec(memory_space=pltpu.VMEM)
    anywhere = pl.BlockSpec(memory_space=pl.ANY)
    specs = [vmem] * len(feats) + [anywhere] + [vmem] * len(params)
    scratch = [
        pltpu.VMEM((d, leads, lanes), f32),
        pltpu.VMEM(bands.shape, bf16),
        pltpu.SemaphoreType.DMA((d // 16,)),
        pltpu.VMEM((2, leads, lanes), f32),
    ]
    if head is None:
        return pl.pallas_call(
            functools.partial(block_body, index, False),
            out_shape=feature_shapes(leads, d),
            in_specs=specs,
            scratch_shapes=scratch + [pltpu.VMEM((leads // 16, d, lanes), bf16)],
            name="block",
            **params_for(44, flops, 20 * leads * d * lanes),
        )(*operands)
    c_out = head.shape[0]
    scratch += [pltpu.VMEM((c_out, leads, lanes), f32), pltpu.SemaphoreType.DMA((leads // 8,))]
    return pl.pallas_call(
        functools.partial(block_body, index, True),
        out_shape=jax.ShapeDtypeStruct((c_out, leads, lanes), f32),
        in_specs=specs + [vmem],
        out_specs=anywhere,
        scratch_shapes=scratch,
        name="block_head",
        **params_for(44, flops, 20 * leads * d * lanes),
    )(*operands, head)


def body(
    q_state,
    scales,
    land_mask,
    stem_weight,
    stem_bias,
    dw_weight,
    dw_bias,
    ln_gain,
    ln_bias,
    w_in,
    b_in,
    w_out,
    b_out,
    layer_scale,
    head_weight,
):
    n_lat = lax.axis_size("lat")
    n_lon = lax.axis_size("lon")
    rows = land_mask.shape[0]
    span = rows // 2
    axes = ("lat", "lon")

    send = prep(q_state, scales, n_lat, n_lon, rows)
    state = lax.all_to_all(send, axes, split_axis=0, concat_axis=0, tiled=True)
    state = state.reshape(-1, rows, lanes)

    mask = land_mask.astype(f32).reshape(2, span, half, 2).transpose(3, 1, 0, 2)
    mask = mask.reshape(rows, lanes)
    d = stem_weight.shape[1]
    thin = jnp.stack([dw_bias, ln_gain, ln_bias], axis=1).reshape(6, d)
    thin = jnp.broadcast_to(thin[:, :, None, None], (6, d, 1, lanes))
    wide = jnp.stack([layer_scale * 0.5, layer_scale * b_out], axis=1).reshape(4, d)
    wide = jnp.concatenate([wide, stem_bias[None]], axis=0)
    wide = jnp.broadcast_to(wide[:, :, None], (5, d, lanes))
    high = b_in.astype(bf16)
    rest = b_in - high.astype(f32)
    mid = rest.astype(bf16)
    low = (rest - mid.astype(f32)).astype(bf16)
    terms = jnp.pad(jnp.stack([high, mid, low], axis=2), ((0, 0), (0, 0), (0, 13)))
    w1 = jnp.concatenate([w_in.transpose(0, 2, 1), terms], axis=2)
    w2 = w_out.transpose(0, 2, 1)
    band_at = lax.axis_index("lat")
    edge = jnp.stack([band_at > 0, band_at < n_lat - 1]).astype(bf16)
    edge = jnp.broadcast_to(edge[:, None, None], (2, 16, lanes))
    dw_weight, ready = lax.optimization_barrier(
        (dw_weight, (thin, wide, w1, w2, stem_weight.T, mask, edge, head_weight.T))
    )
    bands = [band(dw_weight[b], span) for b in range(2)]
    state, bands, (thin, wide, w1, w2, weight_t, mask, edge, head_t) = lax.optimization_barrier(
        (state, bands, ready)
    )

    def shift(x, axis, by):
        n = lax.axis_size(axis)
        return lax.ppermute(x, axis, [(i, (i + by) % n) for i in range(n)])

    def exchange(feat, to_west, to_east, to_south, to_north):
        from_west, from_east = shift(to_east, "lon", 1), shift(to_west, "lon", -1)
        to_south, to_north = rows_with_ends(from_west, from_east, to_south, to_north)
        return feat, from_west, from_east, shift(to_south, "lat", 1), shift(to_north, "lat", -1)

    feats = stem(state, weight_t, wide, mask)
    feats = block(0, exchange(*feats), bands[0], (thin, wide, w1[0], w2[0], mask, edge))
    return block(1, exchange(*feats), bands[1], (thin, wide, w1[1], w2[1], mask, edge), head_t)


def solution(mesh):
    placed = (
        P(("lat", "lon"), None, None),
        P(("lat", "lon"), None),
        P("lat", "lon"),
        *([P()] * 12),
    )
    return jax.shard_map(
        body, mesh=mesh, in_specs=placed, out_specs=P(None, "lat", "lon"), check_vma=False
    )
```

```python
import functools

import jax
import jax.numpy as jnp
import numpy as np
from jax import lax
from jax.experimental import pallas as pl
from jax.experimental.pallas import tpu as pltpu
from jax.sharding import PartitionSpec as P

ln_eps = 1e-06
f32 = jnp.float32
bf16 = jnp.bfloat16
lanes = 128
half = lanes // 2
mib = 2**20


halo_chunk = -1


def window_of(span):
    per = span // 16
    even, odd = list(range(per)), list(range(per, 2 * per))
    order = []
    for s in range(-2, 3):
        chunks = (even if s > -2 else []) + (odd if s < 2 else []) + [halo_chunk]
        order += [(s, c) for c in chunks]
    return order


def window_tables(span):
    per = span // 16
    cols, rows = [], []
    for s, c in window_of(span):
        if c == halo_chunk:
            for phase in range(2):
                cols += [2 * s + phase] * 8
                rows += [-3, -2, -1, span, span + 1, span + 2, 10000, 10000]
        else:
            cols += [2 * s + c // per] * 16
            rows += [16 * (c % per) + q for q in range(16)]
    return np.array([cols], np.int32), np.array([rows], np.int32)


def params_for(vmem, flops=0, bytes_accessed=0):
    return dict(
        compiler_params=pltpu.CompilerParams(vmem_limit_bytes=vmem * mib),
        cost_estimate=pl.CostEstimate(
            flops=int(flops), bytes_accessed=int(bytes_accessed), transcendentals=0
        ),
    )


def lane_index(shape):
    return lax.broadcasted_iota(jnp.int32, shape, len(shape) - 1)


def row_index(shape):
    return lax.broadcasted_iota(jnp.int32, shape, 0)


def turn(x, amount):
    amount %= lanes
    return pltpu.roll(x, amount, 1) if amount else x


def prep_body(q_ref, before_ref, after_ref, s_ref, o_ref):
    channels, rows, cols = q_ref.shape
    tiles = cols // lanes
    span = rows // 2
    shape = (lanes, 2 * lanes)
    to = lane_index(shape)
    at = to & (lanes - 1)
    phase = (at >> 6) ^ (to >> 7)
    order = (row_index(shape) == 2 * (at & (half - 1)) + phase).astype(f32).astype(bf16)
    left = lane_index((span, lanes)) < half
    first = pl.program_id(0) * rows

    def scale_of(c, start, count):
        every = (count, s_ref.shape[1])
        own = lane_index(every) == row_index(every) + start
        return jnp.sum(jnp.where(own, s_ref[c : c + 1, :], 0.0), axis=1, keepdims=True)

    beyond = [[] for _ in range(tiles)]
    for c in range(channels):
        scale = scale_of(c, first, rows)
        scale_before = scale_of(c, first - 16, 16)
        scale_after = scale_of(c, first + rows, 16)
        parts = []
        for ref, own in ((q_ref, scale), (before_ref, scale_before), (after_ref, scale_after)):
            for b in range(tiles):
                cut = slice(b * lanes, (b + 1) * lanes)
                parts.append((ref[c, :, cut].astype(f32) * own).astype(bf16))
        y = jnp.dot(jnp.concatenate(parts, axis=0), order, preferred_element_type=f32)
        for b in range(tiles):
            top = y[b * rows : b * rows + span]
            low = y[b * rows + span : (b + 1) * rows]
            even = jnp.where(left, top[:, :lanes], low[:, lanes:])
            odd = jnp.where(left, top[:, lanes:], low[:, :lanes])
            o_ref[0, b, c * rows : c * rows + span] = even.astype(bf16)
            o_ref[0, b, c * rows + span : (c + 1) * rows] = odd.astype(bf16)
            before = tiles * rows + 16 * b
            after = before + 16 * tiles
            beyond[b] += [y[before + 13 : before + 16, :lanes], y[after : after + 3, :lanes]]
    for b in range(tiles):
        o_ref[0, b, channels * rows :] = jnp.concatenate(beyond[b], axis=0).astype(bf16)


def prep(q_state, scales, n_lat, n_lon, rows):
    channels, n_rows, n_cols = q_state.shape
    count = channels * (rows + 6)
    step, last = rows // 16, n_rows // 16 - 1
    return pl.pallas_call(
        prep_body,
        grid=(n_lat,),
        in_specs=[
            pl.BlockSpec((channels, rows, n_cols), lambda a: (0, a, 0)),
            pl.BlockSpec((channels, 16, n_cols), lambda a: (0, jnp.maximum(a * step - 1, 0), 0)),
            pl.BlockSpec((channels, 16, n_cols), lambda a: (0, jnp.minimum(a * step + step, last), 0)),
            pl.BlockSpec((channels, n_rows), lambda a: (0, 0)),
        ],
        out_specs=pl.BlockSpec((1, n_lon, count, lanes), lambda a: (a, 0, 0, 0)),
        out_shape=jax.ShapeDtypeStruct((n_lat, n_lon, count, lanes), bf16),
        name="dequantize",
        **params_for(60, 0, 4 * q_state.size),
    )(q_state, q_state, q_state, scales).reshape(n_lat * n_lon, count, lanes)


def slot_of(shape):
    return ((lane_index(shape) + 2) >> 2) & 15


def pack_edges(packed, lead, slot):
    turned = turn(lead, 4 * slot)
    return jnp.where(slot_of(lead.shape) == slot, turned, packed)


def first_ends(shape):
    return ((lane_index(shape) + 2) & 3) >= 2


def ends_messages(e_ref, west_ref, east_ref):
    first = first_ends(e_ref.shape[1:])
    for i in range(e_ref.shape[0] // 2):
        one, two = e_ref[2 * i], e_ref[2 * i + 1]
        west_ref[i] = jnp.where(first, one, turn(two, -2))
        east_ref[i] = jnp.where(first, turn(two, 2), one)


def messages(f_ref, e_ref, west_ref, east_ref, south_ref, north_ref):
    shape = f_ref.shape[1:]
    span = f_ref.shape[0] // 2
    ends_messages(e_ref, west_ref, east_ref)
    left = lane_index(shape) < half
    for i in range(3):
        r = span - 3 + i
        south_ref[i] = jnp.where(left, turn(f_ref[r], half), f_ref[span + r])
        north_ref[i] = jnp.where(left, f_ref[i], turn(f_ref[span + i], half))


def received_ends(from_west, from_east):
    first = first_ends(from_west[0].shape)
    groups = []
    for west, east in zip(from_west, from_east):
        groups.append(jnp.where(first, east, west))
        groups.append(jnp.where(first, turn(east, 2), turn(west, -2)))
    return groups


def pack_beyond(north, south):
    packed = jnp.zeros(north[0].shape, bf16)
    for i, value in enumerate([*north, *south]):
        packed = pack_edges(packed, value, i)
    return packed


def rows_body(west_in, east_in, north_in, south_in, west_ref, east_ref):
    count = west_in.shape[0]
    packed = pack_beyond([north_in[i] for i in range(3)], [south_in[i] for i in range(3)])
    west_ref[0:count] = west_in[...]
    east_ref[0:count] = east_in[...]
    west_ref[count] = packed
    east_ref[count] = packed


def with_rows(to_west, to_east, from_north, from_south):
    shape = jax.ShapeDtypeStruct((to_west.shape[0] + 1, *to_west.shape[1:]), bf16)
    return pl.pallas_call(
        rows_body,
        out_shape=[shape, shape],
        name="rows",
        **params_for(20, 0, 20 * to_west.size),
    )(to_west, to_east, from_north, from_south)


def stem_body(x_ref, w_ref, wide_ref, mask_ref, f_ref, west_ref, east_ref, north_ref, south_ref, e_ref):
    bias = wide_ref[4]
    senders, count = x_ref.shape[:2]
    leads = f_ref.shape[0]
    channels = count // (leads + 6)

    def features(x, first, n):
        x = jnp.swapaxes(x, 0, 1)
        joined = jnp.concatenate([x[i] for i in range(n)], axis=1).astype(bf16)
        y = jnp.dot(w_ref[...], joined, preferred_element_type=f32)
        for i in range(n):
            value = (y[:, i * lanes : (i + 1) * lanes] + bias) * mask_ref[first + i : first + i + 1, :]
            yield i, value.astype(bf16)

    for g in range(leads // 16):
        packed = jnp.zeros(f_ref.shape[1:], bf16)
        x = jnp.stack(
            [x_ref[:, c * leads + 16 * g : c * leads + 16 * g + 16, :] for c in range(channels)], axis=1
        )
        for i, value in features(x.reshape(senders * channels, 16, lanes), 16 * g, 16):
            f_ref[16 * g + i] = value
            packed = pack_edges(packed, value, i)
        e_ref[g] = packed
    ends_messages(e_ref, west_ref, east_ref)
    beyond = x_ref[:, channels * leads :, :].astype(f32)
    x = jnp.stack([beyond[:, 6 * c : 6 * c + 6, :] for c in range(channels)], axis=1)
    x = jnp.concatenate([x, jnp.zeros((senders, channels, 2, lanes), f32)], axis=2)
    values = [v for _, v in features(x.reshape(senders * channels, 8, lanes), leads, 6)]
    for i in range(3):
        north_ref[i] = values[i]
        south_ref[i] = values[3 + i]
    packed = pack_beyond(values[:3], values[3:])
    west_ref[leads // 32] = packed
    east_ref[leads // 32] = packed


def feature_shapes(leads, d, more=0):
    return [
        jax.ShapeDtypeStruct((n, d, lanes), bf16)
        for n in (leads, leads // 32 + more, leads // 32 + more, 3, 3)
    ]


def stem(state, weight_t, wide, mask, leads):
    d = weight_t.shape[0]
    return pl.pallas_call(
        stem_body,
        out_shape=feature_shapes(leads, d, 1),
        scratch_shapes=[pltpu.VMEM((leads // 16, d, lanes), bf16)],
        name="stem",
        **params_for(24, 2 * d * state.size, 2 * state.size + 2 * leads * d * lanes),
    )(state, weight_t, wide, mask)


def band_body(w_ref, col_ref, row_ref, o_ref):
    k = o_ref.shape[2]
    taps = w_ref.shape[1]
    at = row_index((taps, k))
    made = []
    for q in range(16):
        i = row_ref[...] - (8 * pl.program_id(0) + q % 8) + 3
        j = col_ref[...] - q // 8 + 3
        tap = jnp.where((i >= 0) & (i < 7) & (j >= 0) & (j < 7), 7 * i + j, -1)
        pick = (at == tap).astype(f32).astype(bf16)
        made.append(jnp.dot(w_ref[...], pick, preferred_element_type=f32).astype(bf16))
    o_ref[...] = jnp.swapaxes(jnp.stack(made), 0, 1)


def band(dw, span):
    d = dw.shape[0]
    cols, rows = window_tables(span)
    k = cols.shape[1]
    taps = jnp.pad(dw.reshape(d, 49), ((0, 0), (0, 15))).astype(bf16)
    return pl.pallas_call(
        band_body,
        grid=(span // 8,),
        in_specs=[
            pl.BlockSpec((d, 64), lambda u: (0, 0)),
            pl.BlockSpec((1, k), lambda u: (0, 0)),
            pl.BlockSpec((1, k), lambda u: (0, 0)),
        ],
        out_specs=pl.BlockSpec((d, 16, k), lambda u: (0, u, 0)),
        out_shape=jax.ShapeDtypeStruct((d, 2 * span, k), bf16),
        name="bands",
        **params_for(20, 0, 4 * d * span * k),
    )(taps, jnp.asarray(cols), jnp.asarray(rows))


def block_body(index, head, *refs):
    f_in, west_in, east_in, north_in, south_in, band_ref = refs[:6]
    thin_ref, wide_ref, w1_ref, w2_ref, mask_ref, edge_ref = refs[6:12]
    refs = refs[12:]
    if head:
        head_ref, out_ref, conv_ref, held_ref, band_sems, sum_ref, tend_ref, sems = refs
    else:
        f_ref, *sent_refs, conv_ref, held_ref, band_sems, sum_ref, e_ref = refs
    leads, d = f_in.shape[:2]
    span = leads // 2
    per = span // 16

    def fetch(g):
        cs = pl.ds(g * 16, 16)
        return pltpu.make_async_copy(band_ref.at[cs], held_ref.at[cs], band_sems.at[g])

    for g in range(d // 16):
        fetch(g).start()

    small = (16, lanes)
    left = lane_index(small) < half
    place = lane_index(small) & (half - 1)
    first = first_ends(small)

    def conv_step(g, _):
        cs = pl.ds(pl.multiple_of(g * 16, 16), 16)
        fetch(g).wait()
        zero = jnp.zeros(small, bf16)

        def ends(group, slot):
            return turn(group, half - 4 * slot)

        count = leads // 32
        packs = received_ends(
            [west_in[i, cs, :] for i in range(count)], [east_in[i, cs, :] for i in range(count)]
        )
        norths = [north_in[i, cs, :] * edge_ref[0] for i in range(3)]
        souths = [south_in[i, cs, :] * edge_ref[1] for i in range(3)]
        both = jnp.where(first, east_in[count, cs, :], west_in[count, cs, :])
        before = [ends(both, i) * edge_ref[0] for i in range(3)]
        after = [ends(both, 3 + i) * edge_ref[1] for i in range(3)]
        chunks = {}
        for k in range(leads // 16):
            x = jnp.stack([f_in[16 * k + q, cs, :] for q in range(16)])
            h = jnp.stack([ends(packs[k], q) for q in range(16)])
            chunks[k] = (jnp.swapaxes(x, 0, 1), jnp.swapaxes(h, 0, 1))
        xrow, hrow = [], []
        for phase in range(2):
            for i in range(3):
                r = span - 3 + i
                own = f_in[phase * span + r, cs, :]
                got = norths[i]
                if phase == 0:
                    xrow.append(jnp.where(left, got, turn(own, half)))
                else:
                    xrow.append(turn(jnp.where(left, own, got), half))
                slot = r % 16
                mine = ends(packs[phase * per + r // 16], slot)
                theirs = turn(before[i], half if phase == 0 else 0)
                hrow.append(turn(jnp.where(left, theirs, mine), half))
            for i in range(3):
                own = f_in[phase * span + i, cs, :]
                got = souths[i]
                if phase == 0:
                    xrow.append(turn(jnp.where(left, got, own), half))
                else:
                    xrow.append(jnp.where(left, turn(own, half), got))
                mine = ends(packs[phase * per], i)
                theirs = turn(after[i], 0 if phase == 0 else half)
                hrow.append(turn(jnp.where(left, mine, theirs), half))
            xrow += [zero, zero]
            hrow += [zero, zero]
        chunks[halo_chunk] = tuple(jnp.swapaxes(jnp.stack(v), 0, 1) for v in (xrow, hrow))
        total = squares = 0.0
        for u in range(16):
            taps = []
            for s, c in window_of(span):
                x, h = chunks[c][0][u], chunks[c][1][u]
                if s:
                    past = (place < s) if s > 0 else (place >= half + s)
                    x = turn(jnp.where(past, h, x), -s)
                taps.append(x)
            taps = jnp.concatenate(taps, axis=0)
            y = jnp.dot(held_ref[g * 16 + u], taps, preferred_element_type=f32)
            y = y + dwb[g * 16 + u]
            conv_ref[g * 16 + u] = y
            if u == 0:
                origin = conv_ref[0]
            y = y - origin
            total = total + y
            squares = squares + y * y
        sum_ref[0] += total
        sum_ref[1] += squares
        return 0

    dwb = thin_ref.at[index]
    sum_ref[...] = jnp.zeros_like(sum_ref)

    lax.fori_loop(0, d // 16, conv_step, 0)

    if head:
        shape = (2 * lanes, 2 * lanes)
        to, at = lane_index(shape), row_index(shape)
        col = to & (lanes - 1)
        source = (col & 1) * lanes + (to >> 7) * half + (col >> 1)
        back = (at == source).astype(f32).astype(bf16)
    ones = (row_index((16, 8 * lanes)) < 3).astype(f32).astype(bf16)
    ls, lsb = wide_ref[2 * index], wide_ref[2 * index + 1]
    held = []
    for k in range(leads // 8):
        u, phase = k // 2, k % 2
        lead = phase * span + 8 * u
        if phase == 0:
            cut = slice(8 * k, 8 * k + 16)
            average = sum_ref[0, cut, :] * (1.0 / d)
            variance = sum_ref[1, cut, :] * (1.0 / d) - average * average
            scale = lax.rsqrt(jnp.maximum(variance, 0.0) + ln_eps)
            centered = conv_ref[:, cut, :] - (conv_ref[0, cut, :] + average)
            both_normed = (centered * scale).astype(bf16)
            both_normed = jnp.swapaxes(both_normed, 0, 1)
        normed = both_normed[8 * phase : 8 * phase + 8]
        joined = jnp.concatenate([normed[i] for i in range(8)], axis=1)
        joined = jnp.concatenate([joined, ones], axis=0)
        hidden = jnp.dot(w1_ref[...], joined, preferred_element_type=f32)
        factor = lax.erf(hidden * 0.7071067811865476).astype(bf16)
        hidden = hidden.astype(bf16)
        hidden = hidden + hidden * factor
        projected = jnp.dot(w2_ref[...], hidden, preferred_element_type=f32)
        if not head:
            packed = jnp.zeros((d, lanes), bf16) if lead % 16 == 0 else e_ref[lead // 16]
        for i in range(8):
            ocean = mask_ref[lead + i : lead + i + 1, :]
            branch = projected[:, i * lanes : (i + 1) * lanes] * ls + lsb
            value = ((f_in[lead + i].astype(f32) + branch) * ocean).astype(bf16)
            if head:
                held.append(value)
            else:
                f_ref[lead + i] = value
                packed = pack_edges(packed, value, (lead + i) % 16)
        if not head:
            e_ref[lead // 16] = packed
        elif phase == 1:
            both = [jnp.concatenate([held[i], held[8 + i]], axis=1) for i in range(8)]
            both = jnp.dot(jnp.concatenate(both, axis=0), back, preferred_element_type=f32)
            both = both.astype(bf16)
            for part in range(2):
                cut = slice(part * lanes, (part + 1) * lanes)
                joined = jnp.concatenate([both[i * d : (i + 1) * d, cut] for i in range(8)], axis=1)
                t = jnp.dot(head_ref[...], joined, preferred_element_type=f32)
                t = jnp.stack([t[:, i * lanes : (i + 1) * lanes] for i in range(8)])
                at = part * span + 8 * u
                tend_ref[:, at : at + 8, :] = jnp.swapaxes(t, 0, 1)
                cut = pl.ds(at, 8)
                pltpu.make_async_copy(
                    tend_ref.at[:, cut, :], out_ref.at[:, cut, :], sems.at[at // 8]
                ).start()
            held = []
    if head:
        for at in range(0, leads, 8):
            cut = pl.ds(at, 8)
            pltpu.make_async_copy(
                tend_ref.at[:, cut, :], out_ref.at[:, cut, :], sems.at[at // 8]
            ).wait()
    else:
        messages(f_ref, e_ref, *sent_refs)


def block(index, feats, bands, params, head=None):
    d, leads, k = bands.shape
    hid = params[2].shape[0]
    flops = 2 * leads * lanes * (2 * d * hid + d * k)
    operands = [*feats, bands, *params]
    vmem = pl.BlockSpec(memory_space=pltpu.VMEM)
    anywhere = pl.BlockSpec(memory_space=pl.ANY)
    specs = [vmem] * len(feats) + [anywhere] + [vmem] * len(params)
    scratch = [
        pltpu.VMEM((d, leads, lanes), f32),
        pltpu.VMEM(bands.shape, bf16),
        pltpu.SemaphoreType.DMA((d // 16,)),
        pltpu.VMEM((2, leads, lanes), f32),
    ]
    if head is None:
        return pl.pallas_call(
            functools.partial(block_body, index, False),
            out_shape=feature_shapes(leads, d),
            in_specs=specs,
            scratch_shapes=scratch + [pltpu.VMEM((leads // 16, d, lanes), bf16)],
            name="block",
            **params_for(44, flops, 20 * leads * d * lanes),
        )(*operands)
    c_out = head.shape[0]
    scratch += [pltpu.VMEM((c_out, leads, lanes), f32), pltpu.SemaphoreType.DMA((leads // 8,))]
    return pl.pallas_call(
        functools.partial(block_body, index, True),
        out_shape=jax.ShapeDtypeStruct((c_out, leads, lanes), f32),
        in_specs=specs + [vmem],
        out_specs=anywhere,
        scratch_shapes=scratch,
        name="block_head",
        **params_for(44, flops, 20 * leads * d * lanes),
    )(*operands, head)


def body(
    q_state,
    scales,
    land_mask,
    stem_weight,
    stem_bias,
    dw_weight,
    dw_bias,
    ln_gain,
    ln_bias,
    w_in,
    b_in,
    w_out,
    b_out,
    layer_scale,
    head_weight,
):
    n_lat = lax.axis_size("lat")
    n_lon = lax.axis_size("lon")
    rows = land_mask.shape[0]
    span = rows // 2
    axes = ("lat", "lon")

    send = prep(q_state, scales, n_lat, n_lon, rows)
    state = lax.all_to_all(send, axes, split_axis=0, concat_axis=0, tiled=True)

    def shift(x, axis, by):
        n = lax.axis_size(axis)
        return lax.ppermute(x, axis, [(i, (i + by) % n) for i in range(n)])

    ocean = land_mask.astype(f32)
    mask = ocean.reshape(2, span, half, 2).transpose(3, 1, 0, 2).reshape(rows, lanes)
    beyond = jnp.concatenate(
        [shift(ocean[rows - 3 :], "lat", 1), shift(ocean[:3], "lat", -1), ocean[:2]], axis=0
    )
    beyond = beyond.reshape(8, half, 2).transpose(0, 2, 1).reshape(8, lanes)
    mask = jnp.concatenate([mask, beyond], axis=0)
    d = stem_weight.shape[1]
    thin = jnp.broadcast_to(dw_bias[:, :, None, None], (2, d, 1, lanes))
    wide = jnp.stack([layer_scale * 0.5, layer_scale * b_out], axis=1).reshape(4, d)
    wide = jnp.concatenate([wide, stem_bias[None]], axis=0)
    wide = jnp.broadcast_to(wide[:, :, None], (5, d, lanes))
    w_wide = w_in.astype(f32)
    bias = b_in + jnp.sum(w_wide * ln_bias[:, :, None], axis=1)
    w_scaled = (w_wide * ln_gain[:, :, None]).astype(bf16)
    high = bias.astype(bf16)
    rest = bias - high.astype(f32)
    mid = rest.astype(bf16)
    low = (rest - mid.astype(f32)).astype(bf16)
    terms = jnp.pad(jnp.stack([high, mid, low], axis=2), ((0, 0), (0, 0), (0, 13)))
    w1 = jnp.concatenate([w_scaled.transpose(0, 2, 1), terms], axis=2)
    w2 = w_out.transpose(0, 2, 1)
    mlp = [(w1[b], w2[b]) for b in range(2)]
    band_at = lax.axis_index("lat")
    edge = jnp.stack([band_at > 0, band_at < n_lat - 1]).astype(bf16)
    edge = jnp.broadcast_to(edge[:, None, None], (2, 16, lanes))
    dw_weight, ready = lax.optimization_barrier(
        (dw_weight, (thin, wide, mlp, stem_weight.T, mask, edge, head_weight.T))
    )
    bands = [band(dw_weight[b], span) for b in range(2)]
    state, bands, (thin, wide, mlp, weight_t, mask, edge, head_t) = lax.optimization_barrier(
        (state, bands, ready)
    )

    def columns(feat, to_west, to_east, north, south):
        return feat, shift(to_east, "lon", 1), shift(to_west, "lon", -1), north, south

    def exchange(feat, to_west, to_east, to_south, to_north):
        north, south = shift(to_south, "lat", 1), shift(to_north, "lat", -1)
        to_west, to_east = with_rows(to_west, to_east, north, south)
        return columns(feat, to_west, to_east, north, south)

    feats = columns(*stem(state, weight_t, wide, mask, rows))
    feats = block(0, feats, bands[0], (thin, wide, *mlp[0], mask, edge))
    return block(1, exchange(*feats), bands[1], (thin, wide, *mlp[1], mask, edge), head_t)


def solution(mesh):
    placed = (
        P(("lat", "lon"), None, None),
        P(("lat", "lon"), None),
        P("lat", "lon"),
        *([P()] * 12),
    )
    return jax.shard_map(
        body, mesh=mesh, in_specs=placed, out_specs=P(None, "lat", "lon"), check_vma=False
    )
```

```python
import functools

import jax
import jax.numpy as jnp
import numpy as np
from jax import lax
from jax.experimental import pallas as pl
from jax.experimental.pallas import tpu as pltpu
from jax.sharding import PartitionSpec as P

ln_eps = 1e-06
f32 = jnp.float32
bf16 = jnp.bfloat16
lanes = 128
half = lanes // 2
mib = 2**20


halo_chunk = -1


def window_of(span):
    per = span // 16
    even, odd = list(range(per)), list(range(per, 2 * per))
    order = []
    for s in range(-2, 3):
        chunks = (even if s > -2 else []) + (odd if s < 2 else []) + [halo_chunk]
        order += [(s, c) for c in chunks]
    return order


def window_tables(span):
    per = span // 16
    cols, rows = [], []
    for s, c in window_of(span):
        if c == halo_chunk:
            for phase in range(2):
                cols += [2 * s + phase] * 8
                rows += [-3, -2, -1, span, span + 1, span + 2, 10000, 10000]
        else:
            cols += [2 * s + c // per] * 16
            rows += [16 * (c % per) + q for q in range(16)]
    return np.array([cols], np.int32), np.array([rows], np.int32)


def params_for(vmem, flops=0, bytes_accessed=0):
    return dict(
        compiler_params=pltpu.CompilerParams(vmem_limit_bytes=vmem * mib),
        cost_estimate=pl.CostEstimate(
            flops=int(flops), bytes_accessed=int(bytes_accessed), transcendentals=0
        ),
    )


def lane_index(shape):
    return lax.broadcasted_iota(jnp.int32, shape, len(shape) - 1)


def row_index(shape):
    return lax.broadcasted_iota(jnp.int32, shape, 0)


def turn(x, amount):
    amount %= lanes
    return pltpu.roll(x, amount, 1) if amount else x


def prep_body(q_ref, before_ref, after_ref, s_ref, o_ref):
    channels, rows, cols = q_ref.shape
    tiles = cols // lanes
    span = rows // 2
    shape = (lanes, 2 * lanes)
    to = lane_index(shape)
    at = to & (lanes - 1)
    phase = (at >> 6) ^ (to >> 7)
    order = (row_index(shape) == 2 * (at & (half - 1)) + phase).astype(f32).astype(bf16)
    left = lane_index((span, lanes)) < half
    first = pl.program_id(0) * rows

    def scale_of(c, start, count):
        every = (count, s_ref.shape[1])
        own = lane_index(every) == row_index(every) + start
        return jnp.sum(jnp.where(own, s_ref[c : c + 1, :], 0.0), axis=1, keepdims=True)

    beyond = [[] for _ in range(tiles)]
    for c in range(channels):
        scale = scale_of(c, first, rows)
        scale_before = scale_of(c, first - 16, 16)
        scale_after = scale_of(c, first + rows, 16)
        parts = []
        for ref, own in ((q_ref, scale), (before_ref, scale_before), (after_ref, scale_after)):
            for b in range(tiles):
                cut = slice(b * lanes, (b + 1) * lanes)
                parts.append((ref[c, :, cut].astype(f32) * own).astype(bf16))
        y = jnp.dot(jnp.concatenate(parts, axis=0), order, preferred_element_type=f32)
        for b in range(tiles):
            top = y[b * rows : b * rows + span]
            low = y[b * rows + span : (b + 1) * rows]
            even = jnp.where(left, top[:, :lanes], low[:, lanes:])
            odd = jnp.where(left, top[:, lanes:], low[:, :lanes])
            o_ref[0, b, c * rows : c * rows + span] = even.astype(bf16)
            o_ref[0, b, c * rows + span : (c + 1) * rows] = odd.astype(bf16)
            before = tiles * rows + 16 * b
            after = before + 16 * tiles
            beyond[b] += [y[before + 13 : before + 16, :lanes], y[after : after + 3, :lanes]]
    for b in range(tiles):
        o_ref[0, b, channels * rows :] = jnp.concatenate(beyond[b], axis=0).astype(bf16)


def prep(q_state, scales, n_lat, n_lon, rows):
    channels, n_rows, n_cols = q_state.shape
    count = channels * (rows + 6)
    step, last = rows // 16, n_rows // 16 - 1
    return pl.pallas_call(
        prep_body,
        grid=(n_lat,),
        in_specs=[
            pl.BlockSpec((channels, rows, n_cols), lambda a: (0, a, 0)),
            pl.BlockSpec((channels, 16, n_cols), lambda a: (0, jnp.maximum(a * step - 1, 0), 0)),
            pl.BlockSpec((channels, 16, n_cols), lambda a: (0, jnp.minimum(a * step + step, last), 0)),
            pl.BlockSpec((channels, n_rows), lambda a: (0, 0)),
        ],
        out_specs=pl.BlockSpec((1, n_lon, count, lanes), lambda a: (a, 0, 0, 0)),
        out_shape=jax.ShapeDtypeStruct((n_lat, n_lon, count, lanes), bf16),
        name="dequantize",
        **params_for(60, 0, 4 * q_state.size),
    )(q_state, q_state, q_state, scales).reshape(n_lat * n_lon, count, lanes)


def slot_of(shape):
    return ((lane_index(shape) + 2) >> 2) & 15


def pack_edges(packed, lead, slot):
    turned = turn(lead, 4 * slot)
    return jnp.where(slot_of(lead.shape) == slot, turned, packed)


def first_ends(shape):
    return ((lane_index(shape) + 2) & 3) >= 2


def ends_messages(e_ref, west_ref, east_ref):
    first = first_ends(e_ref.shape[1:])
    for i in range(e_ref.shape[0] // 2):
        one, two = e_ref[2 * i], e_ref[2 * i + 1]
        west_ref[i] = jnp.where(first, one, turn(two, -2))
        east_ref[i] = jnp.where(first, turn(two, 2), one)


def messages(f_ref, e_ref, west_ref, east_ref, south_ref, north_ref):
    shape = f_ref.shape[1:]
    span = f_ref.shape[0] // 2
    ends_messages(e_ref, west_ref, east_ref)
    left = lane_index(shape) < half
    for i in range(3):
        r = span - 3 + i
        south_ref[i] = jnp.where(left, turn(f_ref[r], half), f_ref[span + r])
        north_ref[i] = jnp.where(left, f_ref[i], turn(f_ref[span + i], half))


def received_ends(from_west, from_east):
    first = first_ends(from_west[0].shape)
    groups = []
    for west, east in zip(from_west, from_east):
        groups.append(jnp.where(first, east, west))
        groups.append(jnp.where(first, turn(east, 2), turn(west, -2)))
    return groups


def pack_beyond(north, south):
    packed = jnp.zeros(north[0].shape, bf16)
    for i, value in enumerate([*north, *south]):
        packed = pack_edges(packed, value, i)
    return packed


def rows_body(west_in, east_in, north_in, south_in, west_ref, east_ref):
    count = west_in.shape[0]
    packed = pack_beyond([north_in[i] for i in range(3)], [south_in[i] for i in range(3)])
    west_ref[0:count] = west_in[...]
    east_ref[0:count] = east_in[...]
    west_ref[count] = packed
    east_ref[count] = packed


def with_rows(to_west, to_east, from_north, from_south):
    shape = jax.ShapeDtypeStruct((to_west.shape[0] + 1, *to_west.shape[1:]), bf16)
    return pl.pallas_call(
        rows_body,
        out_shape=[shape, shape],
        name="rows",
        **params_for(20, 0, 20 * to_west.size),
    )(to_west, to_east, from_north, from_south)


def stem_body(x_ref, w_ref, wide_ref, mask_ref, f_ref, west_ref, east_ref, north_ref, south_ref, e_ref):
    bias = wide_ref[4]
    senders, count = x_ref.shape[:2]
    leads = f_ref.shape[0]
    channels = count // (leads + 6)

    def features(x, first, n):
        x = jnp.swapaxes(x, 0, 1)
        joined = jnp.concatenate([x[i] for i in range(n)], axis=1).astype(bf16)
        y = jnp.dot(w_ref[...], joined, preferred_element_type=f32)
        for i in range(n):
            value = (y[:, i * lanes : (i + 1) * lanes] + bias) * mask_ref[first + i : first + i + 1, :]
            yield i, value.astype(bf16)

    for g in range(leads // 16):
        packed = jnp.zeros(f_ref.shape[1:], bf16)
        x = jnp.stack(
            [x_ref[:, c * leads + 16 * g : c * leads + 16 * g + 16, :] for c in range(channels)], axis=1
        )
        for i, value in features(x.reshape(senders * channels, 16, lanes), 16 * g, 16):
            f_ref[16 * g + i] = value
            packed = pack_edges(packed, value, i)
        e_ref[g] = packed
    ends_messages(e_ref, west_ref, east_ref)
    beyond = x_ref[:, channels * leads :, :].astype(f32)
    x = jnp.stack([beyond[:, 6 * c : 6 * c + 6, :] for c in range(channels)], axis=1)
    x = jnp.concatenate([x, jnp.zeros((senders, channels, 2, lanes), f32)], axis=2)
    values = [v for _, v in features(x.reshape(senders * channels, 8, lanes), leads, 6)]
    for i in range(3):
        north_ref[i] = values[i]
        south_ref[i] = values[3 + i]
    packed = pack_beyond(values[:3], values[3:])
    west_ref[leads // 32] = packed
    east_ref[leads // 32] = packed


def feature_shapes(leads, d, more=0):
    return [
        jax.ShapeDtypeStruct((n, d, lanes), bf16)
        for n in (leads, leads // 32 + more, leads // 32 + more, 3, 3)
    ]


def stem(state, weight_t, wide, mask, leads):
    d = weight_t.shape[0]
    return pl.pallas_call(
        stem_body,
        out_shape=feature_shapes(leads, d, 1),
        scratch_shapes=[pltpu.VMEM((leads // 16, d, lanes), bf16)],
        name="stem",
        **params_for(24, 2 * d * state.size, 2 * state.size + 2 * leads * d * lanes),
    )(state, weight_t, wide, mask)


def band_body(w_ref, col_ref, row_ref, o_ref):
    k = o_ref.shape[2]
    taps = w_ref.shape[1]
    at = row_index((taps, k))
    made = []
    for q in range(16):
        i = row_ref[...] - (8 * pl.program_id(0) + q % 8) + 3
        j = col_ref[...] - q // 8 + 3
        tap = jnp.where((i >= 0) & (i < 7) & (j >= 0) & (j < 7), 7 * i + j, -1)
        pick = (at == tap).astype(f32).astype(bf16)
        made.append(jnp.dot(w_ref[...], pick, preferred_element_type=f32).astype(bf16))
    o_ref[...] = jnp.swapaxes(jnp.stack(made), 0, 1)


def band(dw, span):
    d = dw.shape[0]
    cols, rows = window_tables(span)
    k = cols.shape[1]
    taps = jnp.pad(dw.reshape(d, 49), ((0, 0), (0, 15))).astype(bf16)
    return pl.pallas_call(
        band_body,
        grid=(span // 8,),
        in_specs=[
            pl.BlockSpec((d, 64), lambda u: (0, 0)),
            pl.BlockSpec((1, k), lambda u: (0, 0)),
            pl.BlockSpec((1, k), lambda u: (0, 0)),
        ],
        out_specs=pl.BlockSpec((d, 16, k), lambda u: (0, u, 0)),
        out_shape=jax.ShapeDtypeStruct((d, 2 * span, k), bf16),
        name="bands",
        **params_for(20, 0, 4 * d * span * k),
    )(taps, jnp.asarray(cols), jnp.asarray(rows))


def block_body(index, head, *refs):
    f_in, west_in, east_in, north_in, south_in, band_ref = refs[:6]
    thin_ref, wide_ref, w1_ref, w2_ref, mask_ref, edge_ref = refs[6:12]
    refs = refs[12:]
    if head:
        head_ref, out_ref, conv_ref, held_ref, band_sems, sum_ref, tend_ref, sems = refs
    else:
        f_ref, *sent_refs, conv_ref, held_ref, band_sems, sum_ref, e_ref = refs
    leads, d = f_in.shape[:2]
    span = leads // 2
    per = span // 16

    def fetch(g):
        cs = pl.ds(g * 16, 16)
        return pltpu.make_async_copy(band_ref.at[cs], held_ref.at[cs], band_sems.at[g])

    for g in range(d // 16):
        fetch(g).start()

    small = (16, lanes)
    left = lane_index(small) < half
    place = lane_index(small) & (half - 1)
    first = first_ends(small)

    def conv_step(g, _):
        cs = pl.ds(pl.multiple_of(g * 16, 16), 16)
        fetch(g).wait()
        zero = jnp.zeros(small, bf16)

        def ends(group, slot):
            return turn(group, half - 4 * slot)

        count = leads // 32
        packs = received_ends(
            [west_in[i, cs, :] for i in range(count)], [east_in[i, cs, :] for i in range(count)]
        )
        norths = [north_in[i, cs, :] * edge_ref[0] for i in range(3)]
        souths = [south_in[i, cs, :] * edge_ref[1] for i in range(3)]
        both = jnp.where(first, east_in[count, cs, :], west_in[count, cs, :])
        before = [ends(both, i) * edge_ref[0] for i in range(3)]
        after = [ends(both, 3 + i) * edge_ref[1] for i in range(3)]
        chunks = {}
        for k in range(leads // 16):
            x = jnp.stack([f_in[16 * k + q, cs, :] for q in range(16)])
            h = jnp.stack([ends(packs[k], q) for q in range(16)])
            chunks[k] = (jnp.swapaxes(x, 0, 1), jnp.swapaxes(h, 0, 1))
        xrow, hrow = [], []
        for phase in range(2):
            for i in range(3):
                r = span - 3 + i
                own = f_in[phase * span + r, cs, :]
                got = norths[i]
                if phase == 0:
                    xrow.append(jnp.where(left, got, turn(own, half)))
                else:
                    xrow.append(turn(jnp.where(left, own, got), half))
                slot = r % 16
                mine = ends(packs[phase * per + r // 16], slot)
                theirs = turn(before[i], half if phase == 0 else 0)
                hrow.append(turn(jnp.where(left, theirs, mine), half))
            for i in range(3):
                own = f_in[phase * span + i, cs, :]
                got = souths[i]
                if phase == 0:
                    xrow.append(turn(jnp.where(left, got, own), half))
                else:
                    xrow.append(jnp.where(left, turn(own, half), got))
                mine = ends(packs[phase * per], i)
                theirs = turn(after[i], 0 if phase == 0 else half)
                hrow.append(turn(jnp.where(left, mine, theirs), half))
            xrow += [zero, zero]
            hrow += [zero, zero]
        chunks[halo_chunk] = tuple(jnp.swapaxes(jnp.stack(v), 0, 1) for v in (xrow, hrow))
        total = squares = 0.0
        for u in range(16):
            taps = []
            for s, c in window_of(span):
                x, h = chunks[c][0][u], chunks[c][1][u]
                if s:
                    past = (place < s) if s > 0 else (place >= half + s)
                    x = turn(jnp.where(past, h, x), -s)
                taps.append(x)
            taps = jnp.concatenate(taps, axis=0)
            y = jnp.dot(held_ref[g * 16 + u], taps, preferred_element_type=f32)
            y = y + dwb[g * 16 + u]
            conv_ref[g * 16 + u] = y
            if u == 0:
                origin = conv_ref[0]
            y = y - origin
            total = total + y
            squares = squares + y * y
        sum_ref[0] += total
        sum_ref[1] += squares
        return 0

    dwb, gain, lnb = (thin_ref.at[3 * index + i] for i in range(3))
    sum_ref[...] = jnp.zeros_like(sum_ref)

    lax.fori_loop(0, d // 16, conv_step, 0)

    if head:
        shape = (2 * lanes, 2 * lanes)
        to, at = lane_index(shape), row_index(shape)
        col = to & (lanes - 1)
        source = (col & 1) * lanes + (to >> 7) * half + (col >> 1)
        back = (at == source).astype(f32).astype(bf16)
    ones = (row_index((16, 8 * lanes)) < 3).astype(f32).astype(bf16)
    ls, lsb = wide_ref[2 * index], wide_ref[2 * index + 1]
    held = []
    for k in range(leads // 8):
        u, phase = k // 2, k % 2
        lead = phase * span + 8 * u
        if phase == 0:
            cut = slice(8 * k, 8 * k + 16)
            average = sum_ref[0, cut, :] * (1.0 / d)
            variance = sum_ref[1, cut, :] * (1.0 / d) - average * average
            scale = lax.rsqrt(jnp.maximum(variance, 0.0) + ln_eps)
            centered = conv_ref[:, cut, :] - (conv_ref[0, cut, :] + average)
            both_normed = (centered * scale * gain[...] + lnb[...]).astype(bf16)
            both_normed = jnp.swapaxes(both_normed, 0, 1)
        normed = both_normed[8 * phase : 8 * phase + 8]
        joined = jnp.concatenate([normed[i] for i in range(8)], axis=1)
        joined = jnp.concatenate([joined, ones], axis=0)
        hidden = jnp.dot(w1_ref[...], joined, preferred_element_type=f32)
        hidden = (hidden + hidden * lax.erf(hidden * 0.7071067811865476)).astype(bf16)
        projected = jnp.dot(w2_ref[...], hidden, preferred_element_type=f32)
        if not head:
            packed = jnp.zeros((d, lanes), bf16) if lead % 16 == 0 else e_ref[lead // 16]
        for i in range(8):
            ocean = mask_ref[lead + i : lead + i + 1, :]
            branch = projected[:, i * lanes : (i + 1) * lanes] * ls + lsb
            value = ((f_in[lead + i].astype(f32) + branch) * ocean).astype(bf16)
            if head:
                held.append(value)
            else:
                f_ref[lead + i] = value
                packed = pack_edges(packed, value, (lead + i) % 16)
        if not head:
            e_ref[lead // 16] = packed
        elif phase == 1:
            both = [jnp.concatenate([held[i], held[8 + i]], axis=1) for i in range(8)]
            both = jnp.dot(jnp.concatenate(both, axis=0), back, preferred_element_type=f32)
            both = both.astype(bf16)
            for part in range(2):
                cut = slice(part * lanes, (part + 1) * lanes)
                joined = jnp.concatenate([both[i * d : (i + 1) * d, cut] for i in range(8)], axis=1)
                t = jnp.dot(head_ref[...], joined, preferred_element_type=f32)
                t = jnp.stack([t[:, i * lanes : (i + 1) * lanes] for i in range(8)])
                at = part * span + 8 * u
                tend_ref[:, at : at + 8, :] = jnp.swapaxes(t, 0, 1)
                cut = pl.ds(at, 8)
                pltpu.make_async_copy(
                    tend_ref.at[:, cut, :], out_ref.at[:, cut, :], sems.at[at // 8]
                ).start()
            held = []
    if head:
        for at in range(0, leads, 8):
            cut = pl.ds(at, 8)
            pltpu.make_async_copy(
                tend_ref.at[:, cut, :], out_ref.at[:, cut, :], sems.at[at // 8]
            ).wait()
    else:
        messages(f_ref, e_ref, *sent_refs)


def block(index, feats, bands, params, head=None):
    d, leads, k = bands.shape
    hid = params[2].shape[0]
    flops = 2 * leads * lanes * (2 * d * hid + d * k)
    operands = [*feats, bands, *params]
    vmem = pl.BlockSpec(memory_space=pltpu.VMEM)
    anywhere = pl.BlockSpec(memory_space=pl.ANY)
    specs = [vmem] * len(feats) + [anywhere] + [vmem] * len(params)
    scratch = [
        pltpu.VMEM((d, leads, lanes), f32),
        pltpu.VMEM(bands.shape, bf16),
        pltpu.SemaphoreType.DMA((d // 16,)),
        pltpu.VMEM((2, leads, lanes), f32),
    ]
    if head is None:
        return pl.pallas_call(
            functools.partial(block_body, index, False),
            out_shape=feature_shapes(leads, d),
            in_specs=specs,
            scratch_shapes=scratch + [pltpu.VMEM((leads // 16, d, lanes), bf16)],
            name="block",
            **params_for(44, flops, 20 * leads * d * lanes),
        )(*operands)
    c_out = head.shape[0]
    scratch += [pltpu.VMEM((c_out, leads, lanes), f32), pltpu.SemaphoreType.DMA((leads // 8,))]
    return pl.pallas_call(
        functools.partial(block_body, index, True),
        out_shape=jax.ShapeDtypeStruct((c_out, leads, lanes), f32),
        in_specs=specs + [vmem],
        out_specs=anywhere,
        scratch_shapes=scratch,
        name="block_head",
        **params_for(44, flops, 20 * leads * d * lanes),
    )(*operands, head)


def body(
    q_state,
    scales,
    land_mask,
    stem_weight,
    stem_bias,
    dw_weight,
    dw_bias,
    ln_gain,
    ln_bias,
    w_in,
    b_in,
    w_out,
    b_out,
    layer_scale,
    head_weight,
):
    n_lat = lax.axis_size("lat")
    n_lon = lax.axis_size("lon")
    rows = land_mask.shape[0]
    span = rows // 2
    axes = ("lat", "lon")

    send = prep(q_state, scales, n_lat, n_lon, rows)
    state = lax.all_to_all(send, axes, split_axis=0, concat_axis=0, tiled=True)

    def shift(x, axis, by):
        n = lax.axis_size(axis)
        return lax.ppermute(x, axis, [(i, (i + by) % n) for i in range(n)])

    ocean = land_mask.astype(f32)
    mask = ocean.reshape(2, span, half, 2).transpose(3, 1, 0, 2).reshape(rows, lanes)
    beyond = jnp.concatenate(
        [shift(ocean[rows - 3 :], "lat", 1), shift(ocean[:3], "lat", -1), ocean[:2]], axis=0
    )
    beyond = beyond.reshape(8, half, 2).transpose(0, 2, 1).reshape(8, lanes)
    mask = jnp.concatenate([mask, beyond], axis=0)
    d = stem_weight.shape[1]
    thin = jnp.stack([dw_bias, ln_gain, ln_bias], axis=1).reshape(6, d)
    thin = jnp.broadcast_to(thin[:, :, None, None], (6, d, 1, lanes))
    wide = jnp.stack([layer_scale * 0.5, layer_scale * b_out], axis=1).reshape(4, d)
    wide = jnp.concatenate([wide, stem_bias[None]], axis=0)
    wide = jnp.broadcast_to(wide[:, :, None], (5, d, lanes))
    bias = b_in
    high = lax.reduce_precision(bias, 8, 7)
    mid = lax.reduce_precision(bias - high, 8, 7)
    low = bias - high - mid
    terms = jnp.stack([high, mid, low], axis=2).astype(bf16)
    terms = jnp.pad(terms, ((0, 0), (0, 0), (0, 13)))
    w1 = jnp.concatenate([w_in.transpose(0, 2, 1), terms], axis=2)
    w2 = w_out.transpose(0, 2, 1)
    mlp = [(w1[b], w2[b]) for b in range(2)]
    band_at = lax.axis_index("lat")
    edge = jnp.stack([band_at > 0, band_at < n_lat - 1]).astype(bf16)
    edge = jnp.broadcast_to(edge[:, None, None], (2, 16, lanes))
    dw_weight, ready = lax.optimization_barrier(
        (dw_weight, (thin, wide, mlp, stem_weight.T, mask, edge, head_weight.T))
    )
    bands = [band(dw_weight[b], span) for b in range(2)]
    state, bands, (thin, wide, mlp, weight_t, mask, edge, head_t) = lax.optimization_barrier(
        (state, bands, ready)
    )

    def columns(feat, to_west, to_east, north, south):
        return feat, shift(to_east, "lon", 1), shift(to_west, "lon", -1), north, south

    def exchange(feat, to_west, to_east, to_south, to_north):
        north, south = shift(to_south, "lat", 1), shift(to_north, "lat", -1)
        to_west, to_east = with_rows(to_west, to_east, north, south)
        return columns(feat, to_west, to_east, north, south)

    feats = columns(*stem(state, weight_t, wide, mask, rows))
    feats = block(0, feats, bands[0], (thin, wide, *mlp[0], mask, edge))
    return block(1, exchange(*feats), bands[1], (thin, wide, *mlp[1], mask, edge), head_t)


def solution(mesh):
    placed = (
        P(("lat", "lon"), None, None),
        P(("lat", "lon"), None),
        P("lat", "lon"),
        *([P()] * 12),
    )
    return jax.shard_map(
        body, mesh=mesh, in_specs=placed, out_specs=P(None, "lat", "lon"), check_vma=False
    )
```
